32 devices in a mesh: dp: 8 (over y, x, core), vocab: 4 (over z).
Axes of the slice: x: 2, y: 2, z: 4, core: 2. Of those that a mesh axis runs over, the one named last changes fastest.
Arguments:
- hidden_in: bfloat16 [256, 3584], P(None, 'dp'), may hold values from -64 to 64
- pre_gain: float32 [3584], P('dp'), may hold values from 0.1 to 1.9
- gate_weight: bfloat16 [3584, 14336], P('dp', 'vocab'), may hold values from -0.09375 to 0.09375
- up_weight: bfloat16 [3584, 14336], P('dp', 'vocab'), may hold values from -0.09375 to 0.09375
- down_weight: bfloat16 [14336, 3584], P('vocab', 'dp'), may hold values from -0.046875 to 0.046875
- post_gain: float32 [3584], P('dp'), may hold values from 0.1 to 1.9
- final_gain: float32 [3584], P('dp'), may hold values from 0.1 to 1.9
- embedding: bfloat16 [8192, 3584], P(('dp', 'vocab')), may hold values from -0.3984375 to 0.3984375
- teacher_logits: bfloat16 [256, 8192], P('vocab', 'dp'), may hold values from -30 to 30
- target_ids: int32 [256], replicated, may hold values from 0 to 8191
- lengths: int32 [2], replicated, may hold values from 32 to 128, as said below
Outputs:
- loss: float32 [], replicated
- grad_hidden: bfloat16 [256, 3584], P(None, 'dp')
- grad_gate: bfloat16 [3584, 14336], P('dp', 'vocab')
- grad_up: bfloat16 [3584, 14336], P('dp', 'vocab')
- grad_down: bfloat16 [14336, 3584], P('vocab', 'dp')
- grad_embedding: bfloat16 [8192, 3584], P(('dp', 'vocab'))
The draws below stay inside these ranges and needn't reach their ends.
Inputs may be any that keep to these rules, and one draw needn't show every extreme that they name: The first lengths[k] positions of sequence k are tokens, the rest padding; some sequence has all 128.
All inputs are finite; a program needn't handle non-finite values.
Results may differ from the reference program's by a relative error of at most 0.015.
Values may be sent and summed in bfloat16 or wider, within the bound.
A program may use at most 128 MiB of HBM per device.

```python
import math
import jax
import jax.numpy as jnp
import numpy as np
from jax import lax

D = 3584
FF = 14336
LENGTH = 128
SEQS = 2
TOKENS = 256
V = 8192


def draw_hidden_in(key, part):
    key = jax.random.fold_in(key, 3)
    keys = jax.random.split(key, 3)
    ramp = jnp.arange(D, dtype=jnp.float32) / D
    column = jnp.exp(math.log(10.0) * ramp + jax.random.uniform(keys[1], (D,), minval=-0.5, maxval=0.5)) / 9.0
    rowscale = jnp.exp(jax.random.uniform(keys[2], (TOKENS, 1), minval=math.log(0.3), maxval=math.log(3.0)))
    base = jax.random.normal(keys[0], (TOKENS, D))
    return (base * column[None, :] * rowscale).astype(jnp.bfloat16)


def draw_teacher_logits(key, part):
    key = jax.random.fold_in(key, 7)
    keys = jax.random.split(key, 3)
    column = jnp.exp(jax.random.uniform(keys[1], (1, V), minval=0.0, maxval=math.log(10.0)))
    rowscale = jnp.exp(jax.random.uniform(keys[2], (TOKENS, 1), minval=math.log(0.5), maxval=math.log(2.0)))
    base = jax.random.normal(keys[0], (TOKENS, V))
    raw = 0.9 * base * column * rowscale
    return (30.0 * jnp.tanh(raw / 30.0)).astype(jnp.bfloat16)


def draw_lengths(key, part):
    key = jax.random.fold_in(key, 11)
    keys = jax.random.split(key, 2)
    drawn = jax.random.randint(keys[0], (SEQS,), LENGTH // 4, LENGTH)
    full_index = jax.random.randint(keys[1], (), 0, SEQS)
    return jnp.where(jnp.arange(SEQS, dtype=jnp.int32) == full_index, LENGTH, drawn).astype(jnp.int32)


def set_ends(entries, stream_key, least, high):
    extent = entries.shape
    index_at = [jax.random.randint(jax.random.fold_in(stream_key, axis), (), 0, extent[axis]) for axis in range(len(extent))]
    entries = entries.at[tuple(index_at)].set(least)
    longest = extent.index(max(extent))
    index_at[longest] = (index_at[longest] + 1) % extent[longest]
    return entries.at[tuple(index_at)].set(high)


def shard_levels(key, dims, cuts, least, largest):
    def one(dim, parts):
        draws = jax.random.uniform(jax.random.fold_in(jax.random.fold_in(key, 6), dim), (parts,), jnp.float32, least / len(cuts), largest / len(cuts))
        return jnp.repeat(jnp.exp(draws), dims[dim] // parts).reshape((-1,) + (1,) * (len(dims) - dim - 1))

    level = one(*cuts[0])
    for cut in cuts[1:]:
        level = level * one(*cut)
    return level


def cumulative_ranks(amount, lean):
    weights = [(1 << 20) // math.isqrt(rank ** lean) + 1 for rank in range(1, amount + 1)]
    width = 1 + sum(weights) // (1 << 30)
    return np.cumsum(np.array([max(1, weight // width) for weight in weights]))


def ranked(rng, shape, count, slope):
    table = cumulative_ranks(count, slope)
    pick = jax.random.randint(jax.random.fold_in(rng, 1), shape, 0, int(table[count - 1]))
    grade = jnp.searchsorted(jnp.asarray(table, jnp.int32), pick, side="right")
    return jax.random.permutation(jax.random.fold_in(rng, 2), count)[grade].astype(jnp.int32)


def scatter_about(stream_key, shape, width, most, shards=(), kind=jnp.bfloat16):
    level = shard_levels(stream_key, shape, shards, -0.22, 0.18) if shards else 1.0
    array = jax.random.normal(stream_key, shape, jnp.float32) * width * level
    return jnp.minimum(jnp.maximum(array, -most), most).astype(kind)


def setup_inputs(seed: int = 0) -> dict:
    arg_keys = jax.random.split(jax.random.key(seed), 12)
    hidden_in = draw_hidden_in(jax.random.fold_in(arg_keys[11], 71), 0)
    pre_gain = jnp.clip(1.0 + 0.18 * jax.random.normal(arg_keys[1], (D,), jnp.float32), 0.1, 1.9)
    gate_weight = scatter_about(arg_keys[2], (D, FF), D ** -0.5, 0.09375, ((0, 8), (1, 4)))
    up_weight = scatter_about(arg_keys[3], (D, FF), D ** -0.5, 0.09375, ((0, 8), (1, 4)))
    down_weight = scatter_about(arg_keys[4], (FF, D), FF ** -0.5, 0.046875, ((0, 4), (1, 8)))
    post_gain = jnp.clip(1.0 + 0.18 * jax.random.normal(arg_keys[5], (D,), jnp.float32), 0.1, 1.9)
    final_gain = jnp.clip(1.0 + 0.18 * jax.random.normal(arg_keys[6], (D,), jnp.float32), 0.1, 1.9)
    embedding = scatter_about(arg_keys[7], (V, D), 0.067, 0.3984375, ((0, 32),))
    teacher_logits = draw_teacher_logits(jax.random.fold_in(arg_keys[11], 71), 0)
    target_ids = set_ends(ranked(arg_keys[9], (TOKENS,), V, 2), jax.random.fold_in(arg_keys[9], 3), 0, V - 1).astype(jnp.int32)
    lengths = draw_lengths(jax.random.fold_in(arg_keys[11], 71), 0)
    return dict(hidden_in=hidden_in, pre_gain=pre_gain, gate_weight=gate_weight, up_weight=up_weight, down_weight=down_weight, post_gain=post_gain, final_gain=final_gain, embedding=embedding, teacher_logits=teacher_logits, target_ids=target_ids, lengths=lengths)


eps = 1e-06
softcap_value = 30.0
hard_weight = 0.5
loss_scale = 131072.0

def gelu_tanh(value):
    return jax.nn.gelu(value, approximate=True)

def token_mask(lengths):
    positions = jnp.arange(TOKENS, dtype=jnp.int32)
    sequence = positions // LENGTH
    within = positions % LENGTH
    match = sequence[:, None] == jnp.arange(SEQS, dtype=jnp.int32)[None, :]
    limit = lax.optimization_barrier(jnp.sum(jnp.where(match, lengths[None, :], 0), axis=1))
    return jnp.where(within < limit, 1.0, 0.0).astype(jnp.float32)

def reference(hidden_in, pre_gain, gate_weight, up_weight, down_weight, post_gain, final_gain, embedding, teacher_logits, target_ids, lengths):
    xf = hidden_in.astype(jnp.float32)
    rms_in = lax.rsqrt(lax.optimization_barrier(jnp.mean(xf * xf, axis=1, keepdims=True)) + eps)
    z = (xf * rms_in * pre_gain).astype(jnp.bfloat16)
    gate = jnp.dot(z, gate_weight, preferred_element_type=jnp.float32)
    up = jnp.dot(z, up_weight, preferred_element_type=jnp.float32)
    act, gelu_back = jax.vjp(gelu_tanh, gate)
    hidden = (act * up).astype(jnp.bfloat16)
    branch = jnp.dot(hidden, down_weight, preferred_element_type=jnp.float32)
    rms_br = lax.rsqrt(lax.optimization_barrier(jnp.mean(branch * branch, axis=1, keepdims=True)) + eps)
    stream = xf + branch * rms_br * post_gain
    rms_st = lax.rsqrt(lax.optimization_barrier(jnp.mean(stream * stream, axis=1, keepdims=True)) + eps)
    normed = (stream * rms_st * final_gain).astype(jnp.bfloat16)
    raw = jnp.dot(normed, embedding.T, preferred_element_type=jnp.float32)
    student = softcap_value * jnp.tanh(raw / softcap_value)
    teacher = teacher_logits.astype(jnp.float32)
    exp_s = jnp.exp(student)
    exp_t = jnp.exp(teacher)
    onehot = jnp.where(target_ids[:, None] == jnp.arange(V, dtype=jnp.int32)[None, :], 1.0, 0.0).astype(jnp.float32)
    total_s = lax.optimization_barrier(jnp.sum(exp_s, axis=1))
    total_t = lax.optimization_barrier(jnp.sum(exp_t, axis=1))
    weighted = lax.optimization_barrier(jnp.sum(exp_t * (teacher - student), axis=1))
    picked = lax.optimization_barrier(jnp.sum(onehot * student, axis=1))
    log_s = jnp.log(total_s)
    log_t = jnp.log(total_t)
    mask = token_mask(lengths)
    count = jnp.sum(lengths).astype(jnp.float32)
    per_token = weighted / total_t - log_t + log_s + hard_weight * (log_s - picked)
    loss = jnp.sum(mask * per_token) / count
    factor = loss_scale / count * mask[:, None]
    dstudent = factor * ((1.0 + hard_weight) * exp_s / total_s[:, None] - exp_t / total_t[:, None] - hard_weight * onehot)
    capped = student / softcap_value
    dlogit = (dstudent * (1.0 - capped * capped)).astype(jnp.bfloat16)
    grad_embedding = jnp.dot(dlogit.T, normed, preferred_element_type=jnp.float32).astype(jnp.bfloat16)
    dnormed = jnp.dot(dlogit, embedding, preferred_element_type=jnp.float32)
    along = dnormed * final_gain
    dstream = rms_st * along - stream * rms_st ** 3 * lax.optimization_barrier(jnp.mean(stream * along, axis=1, keepdims=True))
    back = dstream * post_gain
    dbranch = rms_br * back - branch * rms_br ** 3 * lax.optimization_barrier(jnp.mean(branch * back, axis=1, keepdims=True))
    dy = dbranch.astype(jnp.bfloat16)
    grad_down = jnp.dot(hidden.T, dy, preferred_element_type=jnp.float32).astype(jnp.bfloat16)
    dh = jnp.dot(dy, down_weight.T, preferred_element_type=jnp.float32)
    dgate = gelu_back(dh * up)[0].astype(jnp.bfloat16)
    dup = (dh * act).astype(jnp.bfloat16)
    grad_gate = jnp.dot(z.T, dgate, preferred_element_type=jnp.float32).astype(jnp.bfloat16)
    grad_up = jnp.dot(z.T, dup, preferred_element_type=jnp.float32).astype(jnp.bfloat16)
    dz = jnp.dot(dgate, gate_weight.T, preferred_element_type=jnp.float32) + jnp.dot(dup, up_weight.T, preferred_element_type=jnp.float32)
    scaled = dz * pre_gain
    dinput = rms_in * scaled - xf * rms_in ** 3 * lax.optimization_barrier(jnp.mean(xf * scaled, axis=1, keepdims=True))
    grad_hidden = (dstream + dinput).astype(jnp.bfloat16)
    return (loss, grad_hidden, grad_gate, grad_up, grad_down, grad_embedding)
```

```python
import functools
import jax
import jax.numpy as jnp
from jax import lax
from jax.experimental import pallas as pl
from jax.experimental.pallas import tpu as pltpu
from jax.sharding import PartitionSpec as P

D = 3584
LENGTH = 128


eps = 1e-06
softcap_value = 30.0
hard_weight = 0.5
loss_scale = 131072.0


def gelu_tanh(value):
    return jax.nn.gelu(value, approximate=True)


def token_mask(lengths, count):
    positions = jnp.arange(count, dtype=jnp.int32)
    sequence = positions // LENGTH
    within = positions % LENGTH
    match = sequence[:, None] == jnp.arange(lengths.shape[0], dtype=jnp.int32)[None, :]
    limit = jnp.sum(jnp.where(match, lengths[None, :], 0), axis=1)
    return jnp.where(within < limit, 1.0, 0.0).astype(jnp.float32)


def contract_last(left, right):
    return lax.dot_general(
        left, right, (((1,), (1,)), ((), ())), preferred_element_type=jnp.float32
    )


def contract_first(left, right):
    return lax.dot_general(
        left, right, (((0,), (0,)), ((), ())), preferred_element_type=jnp.float32
    )


def on_device_plain(
    hidden_in,
    pre_gain,
    gate_weight,
    up_weight,
    down_weight,
    post_gain,
    final_gain,
    embedding,
    teacher_logits,
    target_ids,
    lengths,
):
    positions = hidden_in.shape[0]
    xf = hidden_in.astype(jnp.float32)
    square_in = lax.psum(jnp.sum(xf * xf, axis=1), "dp")
    rms_in = lax.rsqrt(square_in / D + eps)[:, None]
    z = (xf * rms_in * pre_gain).astype(jnp.bfloat16)
    gate_terms = jnp.dot(z, gate_weight, preferred_element_type=jnp.float32)
    up_terms = jnp.dot(z, up_weight, preferred_element_type=jnp.float32)
    gate, up = lax.psum((gate_terms, up_terms), "dp")
    act, gelu_back = jax.vjp(gelu_tanh, gate)
    hidden = (act * up).astype(jnp.bfloat16)
    branch = lax.psum(jnp.dot(hidden, down_weight, preferred_element_type=jnp.float32), "vocab")
    gained = branch * post_gain
    square_br = lax.psum(jnp.sum(branch * branch, axis=1), "dp")
    rms_br = lax.rsqrt(square_br / D + eps)[:, None]
    stream = xf + gained * rms_br
    square_st = lax.psum(jnp.sum(stream * stream, axis=1), "dp")
    rms_st = lax.rsqrt(square_st / D + eps)[:, None]
    normed_local = (stream * rms_st * final_gain).astype(jnp.bfloat16)
    normed = lax.all_gather(normed_local, "dp", axis=1, tiled=True)
    raw = contract_last(normed, embedding)
    student = softcap_value * jnp.tanh(raw / softcap_value)
    teacher = lax.all_to_all(
        teacher_logits, "vocab", split_axis=1, concat_axis=0, tiled=True
    ).astype(jnp.float32)
    entries = embedding.shape[0]
    columns = lax.axis_index(("dp", "vocab")) * entries + jnp.arange(entries, dtype=jnp.int32)
    onehot = jnp.where(target_ids[:, None] == columns[None, :], 1.0, 0.0).astype(jnp.float32)
    exp_s = jnp.exp(student)
    exp_t = jnp.exp(teacher)
    total_s, total_t, weighted, picked = lax.psum(
        (
            jnp.sum(exp_s, axis=1),
            jnp.sum(exp_t, axis=1),
            jnp.sum(exp_t * (teacher - student), axis=1),
            jnp.sum(onehot * student, axis=1),
        ),
        ("dp", "vocab"),
    )
    log_s = jnp.log(total_s)
    log_t = jnp.log(total_t)
    mask = token_mask(lengths, positions)
    count = jnp.sum(lengths).astype(jnp.float32)
    per_token = weighted / total_t - log_t + log_s + hard_weight * (log_s - picked)
    loss = jnp.sum(mask * per_token) / count
    factor = loss_scale / count * mask[:, None]
    dstudent = factor * (
        (1.0 + hard_weight) * exp_s / total_s[:, None]
        - exp_t / total_t[:, None]
        - hard_weight * onehot
    )
    capped = student / softcap_value
    dlogit = (dstudent * (1.0 - capped * capped)).astype(jnp.bfloat16)
    grad_embedding = contract_first(dlogit, normed).astype(jnp.bfloat16)
    partial_grad = jnp.dot(dlogit, embedding, preferred_element_type=jnp.float32)
    local_grad = lax.psum_scatter(partial_grad, "dp", scatter_dimension=1, tiled=True)
    dnormed = lax.psum(local_grad, "vocab")
    along = dnormed * final_gain
    cube_st = rms_st * rms_st * rms_st
    cube_br = rms_br * rms_br * rms_br
    stream_along = lax.psum(jnp.sum(stream * along, axis=1), "dp")
    dstream = rms_st * along - stream * cube_st * (stream_along[:, None] / D)
    back = dstream * post_gain
    branch_back = lax.psum(jnp.sum(branch * back, axis=1), "dp")
    mean_br = branch_back[:, None] / D
    dbranch = rms_br * back - branch * cube_br * mean_br
    grad_out = dbranch.astype(jnp.bfloat16)
    grad_down = contract_first(hidden, grad_out).astype(jnp.bfloat16)
    dh_terms = contract_last(grad_out, down_weight)
    dh = lax.psum(dh_terms, "dp")
    dgate = gelu_back(dh * up)[0].astype(jnp.bfloat16)
    dup = (dh * act).astype(jnp.bfloat16)
    grad_gate = contract_first(z, dgate).astype(jnp.bfloat16)
    grad_up = contract_first(z, dup).astype(jnp.bfloat16)
    dz = lax.psum(contract_last(dgate, gate_weight) + contract_last(dup, up_weight), "vocab")
    scaled = dz * pre_gain
    input_inner = lax.psum(jnp.sum(xf * scaled, axis=1), "dp")
    cube_in = rms_in * rms_in * rms_in
    dinput = rms_in * scaled - xf * cube_in * (input_inner[:, None] / D)
    grad_hidden = (dstream + dinput).astype(jnp.bfloat16)
    return (loss, grad_hidden, grad_gate, grad_up, grad_down, grad_embedding)


MESH_ID = pl.DeviceIdType.MESH
CUBE = 0.044715
ROOT = 0.7978845608028654
TILE = 512


def vmem():
    return pl.BlockSpec(memory_space=pltpu.VMEM)


def send(src, dst, sems, slot, peer):
    copy = pltpu.make_async_remote_copy(
        src_ref=src,
        dst_ref=dst,
        send_sem=sems.at[0, slot],
        recv_sem=sems.at[1, slot],
        device_id=peer,
        device_id_type=MESH_ID,
    )
    copy.start()
    return copy


def greet(peers):
    barrier = pltpu.get_barrier_semaphore()
    for peer in peers:
        pl.semaphore_signal(barrier, inc=1, device_id=peer, device_id_type=MESH_ID)
    pl.semaphore_wait(barrier, len(peers))


def places(chips):
    dp = lax.axis_index("dp")
    z = lax.axis_index("vocab")
    chip, core = dp // 2, dp % 2
    sibling = (chip * 2 + 1 - core, z)
    others = [(((chip + k) % chips) * 2 + core, z) for k in range(1, chips)]
    return chip, core, sibling, others


def scatter_sum(chips, part, got_pair, out_chip, got_chip, sems, base):
    chip, core, sibling, others = places(chips)
    order = list(range(1, chips)) + [0]
    pair = {}
    for k in order:
        there = (chip + k) % chips
        pair[k] = send(part.at[there, 1 - core], got_pair.at[there], sems, base + k, sibling)
    far = {}
    width = part.shape[-1]
    step = min(TILE, width)
    for k in order:
        there = (chip + k) % chips
        pair[k].wait_recv()
        if k:
            for at in range(0, width, step):
                cols = pl.ds(at, step)
                total = part[there, core, :, cols].astype(jnp.float32) + got_pair[
                    there, :, cols
                ].astype(jnp.float32)
                out_chip[k - 1, :, cols] = total.astype(out_chip.dtype)
            far[k] = send(
                out_chip.at[k - 1], got_chip.at[k - 1], sems, base + chips + k, others[k - 1]
            )
    for k in range(1, chips):
        far[k].wait_recv()

    def take(rows, cols):
        total = part[chip, core, rows, cols].astype(jnp.float32) + got_pair[
            chip, rows, cols
        ].astype(jnp.float32)
        for k in range(1, chips):
            total += got_chip[k - 1, rows, cols].astype(jnp.float32)
        return total

    return take, list(pair.values()) + list(far.values())


def gather_blocks(chips, out, sems, base):
    chip, core, sibling, others = places(chips)
    mine = out.at[chip, core]
    sent = [
        send(mine, mine, sems, base + k, others[k - 1]) for k in range(1, chips)
    ]
    near = send(mine, mine, sems, base, sibling)
    passed = []
    for k in range(1, chips):
        sent[k - 1].wait_recv()
        origin = (chip + chips - k) % chips
        block = out.at[origin, core]
        passed.append(send(block, block, sems, base + chips + k, sibling))
    near.wait_recv()
    for copy in passed:
        copy.wait_recv()
    return sent + [near] + passed


def finish(copies):
    for copy in copies:
        copy.wait_send()


def ffn_kernel(
    chips, rows, x_ref, square_ref, gate_ref, up_ref,
    h_ref, act_ref, slope_ref,
    part, got_pair, out_chip, got_chip, sq, sq_pair, sq_out, sq_chip, sems,
):
    chip, core, sibling, others = places(chips)
    greet([sibling] + others)
    ff = gate_ref.shape[1]
    sq[...] = square_ref[...].reshape(sq.shape)
    for at in range(0, ff, TILE):
        cols = pl.ds(at, TILE)
        for which, weight in ((0, gate_ref), (1, up_ref)):
            terms = jnp.dot(x_ref[...], weight[:, cols], preferred_element_type=jnp.float32)
            part[:, :, pl.ds(which * rows, rows), cols] = terms.astype(jnp.bfloat16).reshape(
                chips, 2, rows, TILE
            )
    take_sq, sent_sq = scatter_sum(chips, sq, sq_pair, sq_out, sq_chip, sems, 0)
    take, sent = scatter_sum(chips, part, got_pair, out_chip, got_chip, sems, 2 * chips)
    rms = lax.rsqrt(take_sq(pl.ds(0, rows), pl.ds(0, 128))[:, :1] / D + eps)
    for at in range(0, ff, TILE):
        cols = pl.ds(at, TILE)
        gate = take(pl.ds(0, rows), cols) * rms
        up = take(pl.ds(rows, rows), cols) * rms
        square = gate * gate
        bend = jnp.tanh(ROOT * (gate + CUBE * gate * square))
        half = 0.5 * (1.0 + bend)
        act = gate * half
        slope = half + 0.5 * gate * (1.0 - bend * bend) * (ROOT * (1.0 + 3.0 * CUBE * square))
        h_ref[chip, core, :, cols] = (act * up).astype(jnp.bfloat16)
        act_ref[:, cols] = act * rms
        slope_ref[:, cols] = up * slope * rms
    finish(sent_sq + sent + gather_blocks(chips, h_ref, sems, 4 * chips))


def ffn_forward(chips, x_gained, squares, gate_weight, up_weight):
    tokens = x_gained.shape[0]
    ff = gate_weight.shape[1]
    rows = tokens // (2 * chips)
    b16, f32 = jnp.bfloat16, jnp.float32
    return pl.pallas_call(
        functools.partial(ffn_kernel, chips, rows),
        out_shape=(
            jax.ShapeDtypeStruct((chips, 2, rows, ff), b16),
            jax.ShapeDtypeStruct((rows, ff), f32),
            jax.ShapeDtypeStruct((rows, ff), f32),
        ),
        in_specs=[vmem()] * 4,
        out_specs=(vmem(),) * 3,
        scratch_shapes=[
            pltpu.VMEM((chips, 2, 2 * rows, ff), b16),
            pltpu.VMEM((chips, 2 * rows, ff), b16),
            pltpu.VMEM((chips - 1, 2 * rows, ff), b16),
            pltpu.VMEM((chips - 1, 2 * rows, ff), b16),
            pltpu.VMEM((chips, 2, rows, 128), f32),
            pltpu.VMEM((chips, rows, 128), f32),
            pltpu.VMEM((chips - 1, rows, 128), f32),
            pltpu.VMEM((chips - 1, rows, 128), f32),
            pltpu.SemaphoreType.DMA((2, 6 * chips)),
        ],
        compiler_params=pltpu.CompilerParams(
            collective_id=1, has_side_effects=True, vmem_limit_bytes=48 * 2**20
        ),
    )(x_gained, squares, gate_weight, up_weight)


def hidden_kernel(
    chips, rows, dy_ref, down_ref, act_ref, slope_ref,
    pair_ref, part, got_pair, out_chip, got_chip, sems,
):
    chip, core, sibling, others = places(chips)
    greet([sibling] + others)
    ff = down_ref.shape[0]
    for at in range(0, ff, TILE):
        cols = pl.ds(at, TILE)
        terms = contract_last(dy_ref[...], down_ref[cols, :])
        part[:, :, :, cols] = terms.astype(jnp.bfloat16).reshape(chips, 2, rows, TILE)
    take, sent = scatter_sum(chips, part, got_pair, out_chip, got_chip, sems, 0)
    for at in range(0, ff, TILE):
        cols = pl.ds(at, TILE)
        dh = take(pl.ds(0, rows), cols)
        pair_ref[chip, core, 0, :, cols] = (dh * slope_ref[:, cols]).astype(jnp.bfloat16)
        pair_ref[chip, core, 1, :, cols] = (dh * act_ref[:, cols]).astype(jnp.bfloat16)
    finish(sent + gather_blocks(chips, pair_ref, sems, 2 * chips))


def hidden_backward(chips, dy, down_weight, act, slope):
    tokens = dy.shape[0]
    ff = down_weight.shape[0]
    rows = tokens // (2 * chips)
    b16 = jnp.bfloat16
    return pl.pallas_call(
        functools.partial(hidden_kernel, chips, rows),
        out_shape=jax.ShapeDtypeStruct((chips, 2, 2, rows, ff), b16),
        in_specs=[vmem()] * 4,
        out_specs=vmem(),
        scratch_shapes=[
            pltpu.VMEM((chips, 2, rows, ff), b16),
            pltpu.VMEM((chips, rows, ff), b16),
            pltpu.VMEM((chips - 1, rows, ff), b16),
            pltpu.VMEM((chips - 1, rows, ff), b16),
            pltpu.SemaphoreType.DMA((2, 4 * chips)),
        ],
        compiler_params=pltpu.CompilerParams(
            collective_id=2, has_side_effects=True, vmem_limit_bytes=48 * 2**20
        ),
    )(dy, down_weight, act, slope)


def on_device(
    chips,
    hidden_in,
    pre_gain,
    gate_weight,
    up_weight,
    down_weight,
    post_gain,
    final_gain,
    embedding,
    teacher_logits,
    target_ids,
    lengths,
):
    positions = hidden_in.shape[0]
    xf = hidden_in.astype(jnp.float32)
    x_gained = (xf * pre_gain).astype(jnp.bfloat16)
    square_local = jnp.sum(xf * xf, axis=1)
    h_blocks, act, slope = ffn_forward(
        chips,
        x_gained,
        jnp.broadcast_to(square_local[:, None], (positions, 128)),
        gate_weight,
        up_weight,
    )
    hidden = h_blocks.reshape(positions, -1)
    branch = lax.psum(jnp.dot(hidden, down_weight, preferred_element_type=jnp.float32), "vocab")
    gained = branch * post_gain
    square_br = lax.psum(jnp.sum(branch * branch, axis=1), "dp")
    rms_br = lax.rsqrt(square_br / D + eps)[:, None]
    stream = xf + gained * rms_br
    square_st = lax.psum(jnp.sum(stream * stream, axis=1), "dp")
    rms_st = lax.rsqrt(square_st / D + eps)[:, None]
    normed_local = (stream * rms_st * final_gain).astype(jnp.bfloat16)
    normed = lax.all_gather(normed_local, "dp", axis=1, tiled=True)
    raw = contract_last(normed, embedding)
    student = softcap_value * jnp.tanh(raw / softcap_value)
    teacher = lax.all_to_all(
        teacher_logits, "vocab", split_axis=1, concat_axis=0, tiled=True
    ).astype(jnp.float32)
    entries = embedding.shape[0]
    columns = lax.axis_index(("dp", "vocab")) * entries + jnp.arange(entries, dtype=jnp.int32)
    onehot = jnp.where(target_ids[:, None] == columns[None, :], 1.0, 0.0).astype(jnp.float32)
    exp_s = jnp.exp(student)
    exp_t = jnp.exp(teacher)
    total_s, total_t, weighted, picked = lax.psum(
        (
            jnp.sum(exp_s, axis=1),
            jnp.sum(exp_t, axis=1),
            jnp.sum(exp_t * (teacher - student), axis=1),
            jnp.sum(onehot * student, axis=1),
        ),
        ("dp", "vocab"),
    )
    log_s = jnp.log(total_s)
    log_t = jnp.log(total_t)
    mask = token_mask(lengths, positions)
    count = jnp.sum(lengths).astype(jnp.float32)
    per_token = weighted / total_t - log_t + log_s + hard_weight * (log_s - picked)
    loss = jnp.sum(mask * per_token) / count
    factor = loss_scale / count * mask[:, None]
    dstudent = factor * (
        (1.0 + hard_weight) * exp_s / total_s[:, None]
        - exp_t / total_t[:, None]
        - hard_weight * onehot
    )
    capped = student / softcap_value
    dlogit = (dstudent * (1.0 - capped * capped)).astype(jnp.bfloat16)
    grad_embedding = contract_first(dlogit, normed).astype(jnp.bfloat16)
    partial_grad = jnp.dot(dlogit, embedding, preferred_element_type=jnp.float32)
    local_grad = lax.psum_scatter(partial_grad, "dp", scatter_dimension=1, tiled=True)
    dnormed = lax.psum(local_grad, "vocab")
    along = dnormed * final_gain
    cube_st = rms_st * rms_st * rms_st
    cube_br = rms_br * rms_br * rms_br
    stream_along = lax.psum(jnp.sum(stream * along, axis=1), "dp")
    dstream = rms_st * along - stream * cube_st * (stream_along[:, None] / D)
    back = dstream * post_gain
    branch_back = lax.psum(jnp.sum(branch * back, axis=1), "dp")
    mean_br = branch_back[:, None] / D
    dbranch = rms_br * back - branch * cube_br * mean_br
    grad_out = dbranch.astype(jnp.bfloat16)
    pairs = hidden_backward(chips, grad_out, down_weight, act, slope)
    dgate = pairs[:, :, 0].reshape(positions, -1)
    dup = pairs[:, :, 1].reshape(positions, -1)
    grad_down = contract_first(hidden, grad_out).astype(jnp.bfloat16)
    grad_gate = contract_first(x_gained, dgate).astype(jnp.bfloat16)
    grad_up = contract_first(x_gained, dup).astype(jnp.bfloat16)
    dz = lax.psum(contract_last(dgate, gate_weight) + contract_last(dup, up_weight), "vocab")
    scaled = dz * pre_gain
    input_inner, square_in = lax.psum((jnp.sum(xf * scaled, axis=1), square_local), "dp")
    mean_in = 1.0 / (square_in / D + eps) * (input_inner / D)
    grad_hidden = (dstream + scaled - xf * mean_in[:, None]).astype(jnp.bfloat16)
    return (loss, grad_hidden, grad_gate, grad_up, grad_down, grad_embedding)


def pick_plan(mesh):
    chips = mesh.shape["dp"] // 2
    tokens = LENGTH * 2
    if mesh.shape["dp"] % 2 == 0 and chips > 1 and tokens % (32 * chips) == 0:
        return functools.partial(on_device, chips)
    return on_device_plain


def solution(mesh):
    return jax.shard_map(
        pick_plan(mesh),
        mesh=mesh,
        in_specs=(
            P(None, "dp"),
            P("dp"),
            P("dp", "vocab"),
            P("dp", "vocab"),
            P("vocab", "dp"),
            P("dp"),
            P("dp"),
            P(("dp", "vocab"), None),
            P("vocab", "dp"),
            P(),
            P(),
        ),
        out_specs=(
            P(),
            P(None, "dp"),
            P("dp", "vocab"),
            P("dp", "vocab"),
            P("vocab", "dp"),
            P(("dp", "vocab"), None),
        ),
        check_vma=False,
    )
```

```python
import functools
import jax
import jax.numpy as jnp
from jax import lax
from jax.experimental import pallas as pl
from jax.experimental.pallas import tpu as pltpu
from jax.sharding import PartitionSpec as P

D = 3584
LENGTH = 128


eps = 1e-06
softcap_value = 30.0
hard_weight = 0.5
loss_scale = 131072.0


def gelu_tanh(value):
    return jax.nn.gelu(value, approximate=True)


def token_mask(lengths, count):
    positions = jnp.arange(count, dtype=jnp.int32)
    sequence = positions // LENGTH
    within = positions % LENGTH
    match = sequence[:, None] == jnp.arange(lengths.shape[0], dtype=jnp.int32)[None, :]
    limit = jnp.sum(jnp.where(match, lengths[None, :], 0), axis=1)
    return jnp.where(within < limit, 1.0, 0.0).astype(jnp.float32)


def contract_last(left, right):
    return lax.dot_general(
        left, right, (((1,), (1,)), ((), ())), preferred_element_type=jnp.float32
    )


def contract_first(left, right):
    return lax.dot_general(
        left, right, (((0,), (0,)), ((), ())), preferred_element_type=jnp.float32
    )


def on_device_plain(
    hidden_in,
    pre_gain,
    gate_weight,
    up_weight,
    down_weight,
    post_gain,
    final_gain,
    embedding,
    teacher_logits,
    target_ids,
    lengths,
):
    positions = hidden_in.shape[0]
    xf = hidden_in.astype(jnp.float32)
    square_in = lax.psum(jnp.sum(xf * xf, axis=1), "dp")
    rms_in = lax.rsqrt(square_in / D + eps)[:, None]
    z = (xf * rms_in * pre_gain).astype(jnp.bfloat16)
    gate_terms = jnp.dot(z, gate_weight, preferred_element_type=jnp.float32)
    up_terms = jnp.dot(z, up_weight, preferred_element_type=jnp.float32)
    gate, up = lax.psum((gate_terms, up_terms), "dp")
    act, gelu_back = jax.vjp(gelu_tanh, gate)
    hidden = (act * up).astype(jnp.bfloat16)
    branch = lax.psum(jnp.dot(hidden, down_weight, preferred_element_type=jnp.float32), "vocab")
    gained = branch * post_gain
    square_br = lax.psum(jnp.sum(branch * branch, axis=1), "dp")
    rms_br = lax.rsqrt(square_br / D + eps)[:, None]
    stream = xf + gained * rms_br
    square_st = lax.psum(jnp.sum(stream * stream, axis=1), "dp")
    rms_st = lax.rsqrt(square_st / D + eps)[:, None]
    normed_local = (stream * rms_st * final_gain).astype(jnp.bfloat16)
    normed = lax.all_gather(normed_local, "dp", axis=1, tiled=True)
    raw = contract_last(normed, embedding)
    student = softcap_value * jnp.tanh(raw / softcap_value)
    teacher = lax.all_to_all(
        teacher_logits, "vocab", split_axis=1, concat_axis=0, tiled=True
    ).astype(jnp.float32)
    entries = embedding.shape[0]
    columns = lax.axis_index(("dp", "vocab")) * entries + jnp.arange(entries, dtype=jnp.int32)
    onehot = jnp.where(target_ids[:, None] == columns[None, :], 1.0, 0.0).astype(jnp.float32)
    exp_s = jnp.exp(student)
    exp_t = jnp.exp(teacher)
    total_s, total_t, weighted, picked = lax.psum(
        (
            jnp.sum(exp_s, axis=1),
            jnp.sum(exp_t, axis=1),
            jnp.sum(exp_t * (teacher - student), axis=1),
            jnp.sum(onehot * student, axis=1),
        ),
        ("dp", "vocab"),
    )
    log_s = jnp.log(total_s)
    log_t = jnp.log(total_t)
    mask = token_mask(lengths, positions)
    count = jnp.sum(lengths).astype(jnp.float32)
    per_token = weighted / total_t - log_t + log_s + hard_weight * (log_s - picked)
    loss = jnp.sum(mask * per_token) / count
    factor = loss_scale / count * mask[:, None]
    dstudent = factor * (
        (1.0 + hard_weight) * exp_s / total_s[:, None]
        - exp_t / total_t[:, None]
        - hard_weight * onehot
    )
    capped = student / softcap_value
    dlogit = (dstudent * (1.0 - capped * capped)).astype(jnp.bfloat16)
    grad_embedding = contract_first(dlogit, normed).astype(jnp.bfloat16)
    partial_grad = jnp.dot(dlogit, embedding, preferred_element_type=jnp.float32)
    local_grad = lax.psum_scatter(partial_grad, "dp", scatter_dimension=1, tiled=True)
    dnormed = lax.psum(local_grad, "vocab")
    along = dnormed * final_gain
    cube_st = rms_st * rms_st * rms_st
    cube_br = rms_br * rms_br * rms_br
    stream_along = lax.psum(jnp.sum(stream * along, axis=1), "dp")
    dstream = rms_st * along - stream * cube_st * (stream_along[:, None] / D)
    back = dstream * post_gain
    branch_back = lax.psum(jnp.sum(branch * back, axis=1), "dp")
    mean_br = branch_back[:, None] / D
    dbranch = rms_br * back - branch * cube_br * mean_br
    grad_out = dbranch.astype(jnp.bfloat16)
    grad_down = contract_first(hidden, grad_out).astype(jnp.bfloat16)
    dh_terms = contract_last(grad_out, down_weight)
    dh = lax.psum(dh_terms, "dp")
    dgate = gelu_back(dh * up)[0].astype(jnp.bfloat16)
    dup = (dh * act).astype(jnp.bfloat16)
    grad_gate = contract_first(z, dgate).astype(jnp.bfloat16)
    grad_up = contract_first(z, dup).astype(jnp.bfloat16)
    dz = lax.psum(contract_last(dgate, gate_weight) + contract_last(dup, up_weight), "vocab")
    scaled = dz * pre_gain
    input_inner = lax.psum(jnp.sum(xf * scaled, axis=1), "dp")
    cube_in = rms_in * rms_in * rms_in
    dinput = rms_in * scaled - xf * cube_in * (input_inner[:, None] / D)
    grad_hidden = (dstream + dinput).astype(jnp.bfloat16)
    return (loss, grad_hidden, grad_gate, grad_up, grad_down, grad_embedding)


MESH_ID = pl.DeviceIdType.MESH
CUBE = 0.044715
ROOT = 0.7978845608028654
TILE = 512


def vmem():
    return pl.BlockSpec(memory_space=pltpu.VMEM)


def send(src, dst, sems, slot, peer):
    copy = pltpu.make_async_remote_copy(
        src_ref=src,
        dst_ref=dst,
        send_sem=sems.at[0, slot],
        recv_sem=sems.at[1, slot],
        device_id=peer,
        device_id_type=MESH_ID,
    )
    copy.start()
    return copy


def greet(peers):
    barrier = pltpu.get_barrier_semaphore()
    for peer in peers:
        pl.semaphore_signal(barrier, inc=1, device_id=peer, device_id_type=MESH_ID)
    pl.semaphore_wait(barrier, len(peers))


def places(chips):
    dp = lax.axis_index("dp")
    z = lax.axis_index("vocab")
    chip, core = dp // 2, dp % 2
    sibling = (chip * 2 + 1 - core, z)
    others = [(((chip + k) % chips) * 2 + core, z) for k in range(1, chips)]
    return chip, core, sibling, others


def scatter_sum(chips, part, got_pair, out_chip, got_chip, sems, base):
    chip, core, sibling, others = places(chips)
    order = list(range(1, chips)) + [0]
    pair = {}
    for k in order:
        there = (chip + k) % chips
        pair[k] = send(part.at[there, 1 - core], got_pair.at[there], sems, base + k, sibling)
    far = {}
    width = part.shape[-1]
    step = min(TILE, width)
    for k in order:
        there = (chip + k) % chips
        pair[k].wait_recv()
        if k:
            for at in range(0, width, step):
                cols = pl.ds(at, step)
                total = part[there, core, :, cols].astype(jnp.float32) + got_pair[
                    there, :, cols
                ].astype(jnp.float32)
                out_chip[k - 1, :, cols] = total.astype(out_chip.dtype)
            far[k] = send(
                out_chip.at[k - 1], got_chip.at[k - 1], sems, base + chips + k, others[k - 1]
            )
    for k in range(1, chips):
        far[k].wait_recv()

    def take(rows, cols):
        total = part[chip, core, rows, cols].astype(jnp.float32) + got_pair[
            chip, rows, cols
        ].astype(jnp.float32)
        for k in range(1, chips):
            total += got_chip[k - 1, rows, cols].astype(jnp.float32)
        return total

    return take, list(pair.values()) + list(far.values())


def gather_blocks(chips, out, sems, base):
    chip, core, sibling, others = places(chips)
    mine = out.at[chip, core]
    sent = [
        send(mine, mine, sems, base + k, others[k - 1]) for k in range(1, chips)
    ]
    near = send(mine, mine, sems, base, sibling)
    passed = []
    for k in range(1, chips):
        sent[k - 1].wait_recv()
        origin = (chip + chips - k) % chips
        block = out.at[origin, core]
        passed.append(send(block, block, sems, base + chips + k, sibling))
    near.wait_recv()
    for copy in passed:
        copy.wait_recv()
    return sent + [near] + passed


def finish(copies):
    for copy in copies:
        copy.wait_send()


def ffn_kernel(
    chips, rows, x_ref, square_ref, gate_ref, up_ref,
    h_ref, act_ref, slope_ref,
    part, got_pair, out_chip, got_chip, sq, sq_pair, sq_out, sq_chip, sems,
):
    chip, core, sibling, others = places(chips)
    greet([sibling] + others)
    ff = gate_ref.shape[1]
    sq[...] = square_ref[...].reshape(sq.shape)
    for at in range(0, ff, TILE):
        cols = pl.ds(at, TILE)
        for which, weight in ((0, gate_ref), (1, up_ref)):
            terms = jnp.dot(x_ref[...], weight[:, cols], preferred_element_type=jnp.float32)
            part[:, :, pl.ds(which * rows, rows), cols] = terms.astype(jnp.bfloat16).reshape(
                chips, 2, rows, TILE
            )
    take_sq, sent_sq = scatter_sum(chips, sq, sq_pair, sq_out, sq_chip, sems, 0)
    take, sent = scatter_sum(chips, part, got_pair, out_chip, got_chip, sems, 2 * chips)
    rms = lax.rsqrt(take_sq(pl.ds(0, rows), pl.ds(0, 128))[:, :1] / D + eps)
    for at in range(0, ff, TILE):
        cols = pl.ds(at, TILE)
        gate = take(pl.ds(0, rows), cols) * rms
        up = take(pl.ds(rows, rows), cols) * rms
        square = gate * gate
        bend = jnp.tanh(ROOT * (gate + CUBE * gate * square))
        half = 0.5 * (1.0 + bend)
        act = gate * half
        slope = half + 0.5 * gate * (1.0 - bend * bend) * (ROOT * (1.0 + 3.0 * CUBE * square))
        h_ref[chip, core, :, cols] = (act * up).astype(jnp.bfloat16)
        act_ref[:, cols] = act * rms
        slope_ref[:, cols] = up * slope * rms
    finish(sent_sq + sent + gather_blocks(chips, h_ref, sems, 4 * chips))


def ffn_forward(chips, x_gained, squares, gate_weight, up_weight):
    tokens = x_gained.shape[0]
    ff = gate_weight.shape[1]
    rows = tokens // (2 * chips)
    b16, f32 = jnp.bfloat16, jnp.float32
    return pl.pallas_call(
        functools.partial(ffn_kernel, chips, rows),
        out_shape=(
            jax.ShapeDtypeStruct((chips, 2, rows, ff), b16),
            jax.ShapeDtypeStruct((rows, ff), f32),
            jax.ShapeDtypeStruct((rows, ff), f32),
        ),
        in_specs=[vmem()] * 4,
        out_specs=(vmem(),) * 3,
        scratch_shapes=[
            pltpu.VMEM((chips, 2, 2 * rows, ff), b16),
            pltpu.VMEM((chips, 2 * rows, ff), b16),
            pltpu.VMEM((chips - 1, 2 * rows, ff), b16),
            pltpu.VMEM((chips - 1, 2 * rows, ff), b16),
            pltpu.VMEM((chips, 2, rows, 128), f32),
            pltpu.VMEM((chips, rows, 128), f32),
            pltpu.VMEM((chips - 1, rows, 128), f32),
            pltpu.VMEM((chips - 1, rows, 128), f32),
            pltpu.SemaphoreType.DMA((2, 6 * chips)),
        ],
        compiler_params=pltpu.CompilerParams(
            collective_id=1, has_side_effects=True, vmem_limit_bytes=48 * 2**20
        ),
    )(x_gained, squares, gate_weight, up_weight)


def hidden_kernel(
    chips, rows, dy_ref, down_ref, act_ref, slope_ref,
    pair_ref, part, got_pair, out_chip, got_chip, sems,
):
    chip, core, sibling, others = places(chips)
    greet([sibling] + others)
    ff = down_ref.shape[0]
    for at in range(0, ff, TILE):
        cols = pl.ds(at, TILE)
        terms = contract_last(dy_ref[...], down_ref[cols, :])
        part[:, :, :, cols] = terms.astype(jnp.bfloat16).reshape(chips, 2, rows, TILE)
    take, sent = scatter_sum(chips, part, got_pair, out_chip, got_chip, sems, 0)
    for at in range(0, ff, TILE):
        cols = pl.ds(at, TILE)
        dh = take(pl.ds(0, rows), cols)
        pair_ref[chip, core, 0, :, cols] = (dh * slope_ref[:, cols]).astype(jnp.bfloat16)
        pair_ref[chip, core, 1, :, cols] = (dh * act_ref[:, cols]).astype(jnp.bfloat16)
    finish(sent + gather_blocks(chips, pair_ref, sems, 2 * chips))


def hidden_backward(chips, dy, down_weight, act, slope):
    tokens = dy.shape[0]
    ff = down_weight.shape[0]
    rows = tokens // (2 * chips)
    b16 = jnp.bfloat16
    return pl.pallas_call(
        functools.partial(hidden_kernel, chips, rows),
        out_shape=jax.ShapeDtypeStruct((chips, 2, 2, rows, ff), b16),
        in_specs=[vmem()] * 4,
        out_specs=vmem(),
        scratch_shapes=[
            pltpu.VMEM((chips, 2, rows, ff), b16),
            pltpu.VMEM((chips, rows, ff), b16),
            pltpu.VMEM((chips - 1, rows, ff), b16),
            pltpu.VMEM((chips - 1, rows, ff), b16),
            pltpu.SemaphoreType.DMA((2, 4 * chips)),
        ],
        compiler_params=pltpu.CompilerParams(
            collective_id=2, has_side_effects=True, vmem_limit_bytes=48 * 2**20
        ),
    )(dy, down_weight, act, slope)


def spots(chips, depth):
    dp = lax.axis_index("dp")
    z = lax.axis_index("vocab")
    chip, core = dp // 2, dp % 2
    group = [(lax.rem(dp + k, 2 * chips), z) for k in range(1, 2 * chips)]
    line = [(dp, lax.rem(z + k, depth)) for k in range(1, depth)]
    others = [(lax.rem(chip + k, chips) * 2 + core, z) for k in range(1, chips)]
    sibling = (chip * 2 + 1 - core, z)
    return dp, z, chip, core, group, line, others, sibling


def feature_sum(value):
    return jnp.sum(jnp.sum(value, axis=0), axis=1, keepdims=True)


def norms(y, side, rows):
    x = side[:, 0:rows, :]
    post = side[:, rows : rows + 1, :]
    final = side[:, rows + 1 : rows + 2, :]
    rms_br = lax.rsqrt(feature_sum(y * y) / D + eps)[None]
    stream = x + y * rms_br * post
    rms_st = lax.rsqrt(feature_sum(stream * stream) / D + eps)[None]
    return stream, rms_br, rms_st, post, final


def branch_kernel(
    chips, depth, h_ref, down_ref, x_ref, gains_ref, teacher_ref,
    normed_ref, y_ref, side_ref, logits_ref,
    side, part, got, total, sems,
):
    dp, z, chip, core, group, line, others, sibling = spots(chips, depth)
    rows = x_ref.shape[2]
    count = 2 * chips
    half = chips
    greet(group + line)
    base = 0
    sent = []
    entries = logits_ref.shape[2]
    tea = []
    for k in range(1, depth):
        cols = pl.ds(pl.multiple_of(lax.rem(z + k, depth) * entries, 128), entries)
        tea.append(send(teacher_ref.at[:, cols], logits_ref.at[z], sems, base + k, line[k - 1]))
    base += depth
    for q in range(chips):
        side[q, 0:rows, :] = x_ref[q, z].astype(jnp.float32)
        side[q, rows : rows + 8, :] = gains_ref[...]
    early = []
    for k in range(1, count):
        there = lax.rem(dp + k, count) // 2
        early.append(send(side.at[there], side_ref.at[dp], sems, base + k, group[k - 1]))
    base += count
    side_ref[dp] = side[chip]
    own = pl.ds(pl.multiple_of(z * entries, 128), entries)
    logits_ref[z] = teacher_ref[:, own]
    terms = jnp.dot(h_ref[...], down_ref[...], preferred_element_type=jnp.float32)
    part[...] = terms.reshape(part.shape)
    down = []
    for k in range(1, depth):
        there = lax.rem(z + k, depth)
        down.append(send(part.at[:, there], got.at[k - 1], sems, base + k, line[k - 1]))
    base += depth
    for copy in down:
        copy.wait_recv()
    summed = part[:, z]
    for k in range(1, depth):
        summed += got[k - 1]
    total[...] = summed
    across = []
    for k in range(1, count):
        there = lax.rem(dp + k, count) // 2
        across.append(send(total.at[there], y_ref.at[dp], sems, base + k, group[k - 1]))
    base += count
    y_ref[dp] = total[chip]
    for copy in early + across:
        copy.wait_recv()
    stream, rms_br, rms_st, post, final = norms(y_ref[...], side_ref[...], rows)
    normed_ref[:, chip, z] = (stream * rms_st * final).astype(jnp.bfloat16)
    mine = pl.ds(core * half, half)
    up = []
    for k in range(1, depth):
        block = normed_ref.at[mine, chip, z]
        up.append(send(block, block, sems, base + k, line[k - 1]))
    base += depth
    wide = []
    passed = []
    for k in range(depth):
        at = lax.rem(z + depth - k, depth)
        block = normed_ref.at[mine, chip, at]
        if k:
            up[k - 1].wait_recv()
            passed.append(send(block, block, sems, base + chips * depth + k, sibling))
        for j in range(1, chips):
            wide.append((j, send(block, block, sems, base + k * chips + j, others[j - 1])))
    base += chips * depth + depth
    for j in range(1, chips):
        for other, copy in wide:
            if other == j:
                copy.wait_recv()
        block = normed_ref.at[mine, lax.rem(chip + chips - j, chips)]
        passed.append(send(block, block, sems, base + j, sibling))
    for copy in passed + tea:
        copy.wait_recv()
    finish(tea + early + down + across + up + passed + [copy for _, copy in wide])


def branch_forward(chips, depth, hidden, down_weight, x_blocks, gains, teacher_logits):
    _, _, rows, features = x_blocks.shape
    entries = teacher_logits.shape[1] // depth
    count = 2 * chips
    f32 = jnp.float32
    return pl.pallas_call(
        functools.partial(branch_kernel, chips, depth),
        out_shape=(
            jax.ShapeDtypeStruct((count, chips, depth, rows, features), jnp.bfloat16),
            jax.ShapeDtypeStruct((count, rows, features), f32),
            jax.ShapeDtypeStruct((count, rows + 8, features), f32),
            jax.ShapeDtypeStruct((depth, teacher_logits.shape[0], entries), jnp.bfloat16),
        ),
        in_specs=[vmem()] * 5,
        out_specs=(vmem(),) * 4,
        scratch_shapes=[
            pltpu.VMEM((chips, rows + 8, features), f32),
            pltpu.VMEM((chips, depth, rows, features), f32),
            pltpu.VMEM((depth - 1, chips, rows, features), f32),
            pltpu.VMEM((chips, rows, features), f32),
            pltpu.SemaphoreType.DMA((2, 4 * depth + 5 * chips + chips * depth)),
        ],
        compiler_params=pltpu.CompilerParams(
            collective_id=3, has_side_effects=True, vmem_limit_bytes=48 * 2**20
        ),
    )(hidden, down_weight, x_blocks, gains, teacher_logits)


def head_kernel(
    chips, depth, normed_ref, emb_ref, teacher_ref, factor_ref, local_ref, y_ref, side_ref,
    stats_ref, grad_emb_ref, dy_ref, back_ref,
    student, exp_s, exp_t, flat, near, dp_stats, z_stats,
    part, got_pair, out_chip, got_chip, line_part, got_line, owned, pay, sems,
):
    dp, z, chip, core, group, line, others, sibling = spots(chips, depth)
    count = 2 * chips
    half = chips
    rows = y_ref.shape[1]
    tokens, entries = teacher_ref.shape
    f32, b16 = jnp.float32, jnp.bfloat16
    greet(group + line)
    raw = contract_last(normed_ref[0], emb_ref[0])
    for d in range(1, count):
        raw += contract_last(normed_ref[d], emb_ref[d])
    logits = softcap_value * jnp.tanh(raw / softcap_value)
    student[...] = logits
    teacher = teacher_ref[...].astype(f32)
    exp_s[...] = jnp.exp(logits)
    exp_t[...] = jnp.exp(teacher)
    hot = local_ref[...] == lax.broadcasted_iota(jnp.int32, (tokens, entries), 1)
    lane = lax.broadcasted_iota(jnp.int32, (tokens, 128), 1)
    sums = [
        jnp.sum(exp_s[...], axis=1, keepdims=True),
        jnp.sum(exp_t[...], axis=1, keepdims=True),
        jnp.sum(exp_t[...] * (teacher - logits), axis=1, keepdims=True),
        jnp.sum(jnp.where(hot, logits, 0.0), axis=1, keepdims=True),
    ]
    columns = jnp.zeros((tokens, 128), f32)
    for i, value in enumerate(sums):
        columns = jnp.where(lane == i, value, columns)
    near[...] = columns.T[0:8, :]
    base = 0
    first = []
    for k in range(1, count):
        first.append(send(near, dp_stats.at[dp], sems, base + k, group[k - 1]))
    base += count
    dp_stats[dp] = near[...]
    for copy in first:
        copy.wait_recv()
    z_stats[z] = jnp.sum(dp_stats[...], axis=0)
    second = []
    for k in range(1, depth):
        second.append(send(z_stats.at[z], z_stats.at[z], sems, base + k, line[k - 1]))
    base += depth
    for copy in second:
        copy.wait_recv()
    whole = jnp.sum(z_stats[...], axis=0)
    stats_ref[...] = whole
    flat[...] = jnp.zeros_like(flat)
    flat[0:8, :] = whole
    columns = flat[...].T
    total_s = columns[:, 0:1]
    total_t = columns[:, 1:2]
    capped = student[...] / softcap_value
    dstudent = factor_ref[...] * (
        exp_s[...] * ((1.0 + hard_weight) / total_s)
        - exp_t[...] / total_t
        - jnp.where(hot, hard_weight, 0.0)
    )
    dlogit = (dstudent * (1.0 - capped * capped)).astype(b16)
    for d in range(count):
        terms = jnp.dot(dlogit, emb_ref[d], preferred_element_type=f32)
        part[d] = terms.astype(b16).reshape(chips, depth, rows, -1)
    theirs = pl.ds((1 - core) * half, half)
    mine = pl.ds(core * half, half)
    order = list(range(1, chips)) + [0]
    pair = {}
    for k in order:
        there = lax.rem(chip + k, chips)
        pair[k] = send(part.at[theirs, there], got_pair.at[:, there], sems, base + k, sibling)
    base += chips
    far = []
    for k in range(1, chips):
        there = lax.rem(chip + k, chips)
        pair[k].wait_recv()
        for i in range(half):
            out_chip[k - 1, i] = (
                part[core * half + i, there].astype(f32) + got_pair[i, there].astype(f32)
            ).astype(b16)
        far.append(send(out_chip.at[k - 1], got_chip.at[k - 1], sems, base + k, others[k - 1]))
    base += chips
    for d in range(count):
        grad_emb_ref[d] = contract_first(dlogit, normed_ref[d]).astype(b16)
    pair[0].wait_recv()
    for copy in far:
        copy.wait_recv()
    for i in range(half):
        value = part[core * half + i, chip].astype(f32) + got_pair[i, chip].astype(f32)
        for k in range(1, chips):
            value += got_chip[k - 1, i].astype(f32)
        line_part[:, i] = value.astype(b16)
    across = []
    for k in range(1, depth):
        there = lax.rem(z + k, depth)
        across.append(send(line_part.at[there], got_line.at[k - 1], sems, base + k, line[k - 1]))
    base += depth
    for copy in across:
        copy.wait_recv()
    value = line_part[z].astype(f32)
    for k in range(1, depth):
        value += got_line[k - 1].astype(f32)
    owned[mine] = value
    swap = send(owned.at[mine], owned.at[mine], sems, base, sibling)
    base += 1
    y = y_ref[...]
    stream, rms_br, rms_st, post, final = norms(y, side_ref[...], rows)
    swap.wait_recv()
    along = owned[...] * final
    mean_st = feature_sum(stream * along)[None] / D
    dstream = rms_st * along - stream * (rms_st * rms_st * rms_st) * mean_st
    back = dstream * post
    mean_br = feature_sum(y * back)[None] / D
    dbranch = rms_br * back - y * (rms_br * rms_br * rms_br) * mean_br
    pay[:, 0] = dbranch.astype(b16)
    pay[:, 1] = dstream.astype(b16)
    home = []
    for k in range(1, chips):
        there = lax.rem(chip + k, chips) * 2 + core
        home.append(send(pay.at[there], back_ref.at[chip], sems, base + k, others[k - 1]))
    base += chips
    back_ref[chip] = pay[dp]
    for copy in home:
        copy.wait_recv()
    dy_ref[:, z] = back_ref[:, 0]
    last = []
    for k in range(1, depth):
        last.append(send(dy_ref.at[:, z], dy_ref.at[:, z], sems, base + k, line[k - 1]))
    for copy in last:
        copy.wait_recv()
    finish(first + second + list(pair.values()) + far + across + [swap] + home + last)


def head_both(chips, depth, normed, emb_blocks, teacher, factor, local, y, side):
    count, tokens, features = normed.shape
    entries = emb_blocks.shape[1]
    rows = y.shape[1]
    f32, b16 = jnp.float32, jnp.bfloat16
    return pl.pallas_call(
        functools.partial(head_kernel, chips, depth),
        out_shape=(
            jax.ShapeDtypeStruct((8, tokens), f32),
            jax.ShapeDtypeStruct((count, entries, features), b16),
            jax.ShapeDtypeStruct((chips, depth, rows, features), b16),
            jax.ShapeDtypeStruct((chips, 2, rows, features), b16),
        ),
        in_specs=[vmem()] * 7,
        out_specs=(vmem(),) * 4,
        scratch_shapes=[
            pltpu.VMEM((tokens, entries), f32),
            pltpu.VMEM((tokens, entries), f32),
            pltpu.VMEM((tokens, entries), f32),
            pltpu.VMEM((128, tokens), f32),
            pltpu.VMEM((8, tokens), f32),
            pltpu.VMEM((count, 8, tokens), f32),
            pltpu.VMEM((depth, 8, tokens), f32),
            pltpu.VMEM((count, chips, depth, rows, features), b16),
            pltpu.VMEM((chips, chips, depth, rows, features), b16),
            pltpu.VMEM((chips - 1, chips, depth, rows, features), b16),
            pltpu.VMEM((chips - 1, chips, depth, rows, features), b16),
            pltpu.VMEM((depth, chips, rows, features), b16),
            pltpu.VMEM((depth - 1, chips, rows, features), b16),
            pltpu.VMEM((count, rows, features), f32),
            pltpu.VMEM((count, 2, rows, features), b16),
            pltpu.SemaphoreType.DMA((2, 5 * chips + 3 * depth + 1)),
        ],
        compiler_params=pltpu.CompilerParams(
            collective_id=4, has_side_effects=True, vmem_limit_bytes=48 * 2**20
        ),
    )(normed, emb_blocks, teacher, factor, local, y, side)


def input_kernel(
    chips, depth, dgate_ref, dup_ref, gate_ref, up_ref, x_ref, gain_ref, back_ref,
    out_ref, part, got, scaled, mine, inner, sems,
):
    dp, z, chip, core, group, line, others, sibling = spots(chips, depth)
    count = 2 * chips
    f32, b16 = jnp.float32, jnp.bfloat16
    rows = x_ref.shape[2]
    greet(group + line)
    dz = contract_last(dgate_ref[...], gate_ref[...]) + contract_last(dup_ref[...], up_ref[...])
    part[...] = (dz * gain_ref[0:1, :]).astype(b16).reshape(part.shape)
    base = 0
    first = []
    for k in range(1, depth):
        there = lax.rem(z + k, depth)
        first.append(send(part.at[:, there], got.at[k - 1], sems, base + k, line[k - 1]))
    base += depth
    for copy in first:
        copy.wait_recv()
    value = part[:, z].astype(f32)
    for k in range(1, depth):
        value += got[k - 1].astype(f32)
    scaled[...] = value
    x = x_ref[:, z].astype(f32)
    lane = lax.broadcasted_iota(jnp.int32, (chips, rows, 128), 2)
    products = jnp.sum(x * value, axis=2, keepdims=True)
    squares = jnp.sum(x * x, axis=2, keepdims=True)
    mine[...] = jnp.where(lane == 0, products, jnp.where(lane == 1, squares, 0.0))
    second = []
    for k in range(1, count):
        second.append(send(mine, inner.at[dp], sems, base + k, group[k - 1]))
    base += count
    inner[dp] = mine[...]
    for copy in second:
        copy.wait_recv()
    sums = jnp.sum(inner[...], axis=0)
    mean = sums[:, :, 0:1] / D / (sums[:, :, 1:2] / D + eps)
    out_ref[:, z] = (back_ref[:, 1].astype(f32) + scaled[...] - x * mean).astype(b16)
    last = []
    for k in range(1, depth):
        last.append(send(out_ref.at[:, z], out_ref.at[:, z], sems, base + k, line[k - 1]))
    for copy in last:
        copy.wait_recv()
    finish(first + second + last)


def input_backward(chips, depth, dgate, dup, gate_weight, up_weight, x_blocks, gain, back):
    _, _, rows, features = x_blocks.shape
    f32, b16 = jnp.float32, jnp.bfloat16
    return pl.pallas_call(
        functools.partial(input_kernel, chips, depth),
        out_shape=jax.ShapeDtypeStruct((chips, depth, rows, features), b16),
        in_specs=[vmem()] * 7,
        out_specs=vmem(),
        scratch_shapes=[
            pltpu.VMEM((chips, depth, rows, features), b16),
            pltpu.VMEM((depth - 1, chips, rows, features), b16),
            pltpu.VMEM((chips, rows, features), f32),
            pltpu.VMEM((chips, rows, 128), f32),
            pltpu.VMEM((2 * chips, chips, rows, 128), f32),
            pltpu.SemaphoreType.DMA((2, 2 * depth + 2 * chips)),
        ],
        compiler_params=pltpu.CompilerParams(
            collective_id=5, has_side_effects=True, vmem_limit_bytes=48 * 2**20
        ),
    )(dgate, dup, gate_weight, up_weight, x_blocks, gain, back)


def on_device(
    chips,
    depth,
    hidden_in,
    pre_gain,
    gate_weight,
    up_weight,
    down_weight,
    post_gain,
    final_gain,
    embedding,
    teacher_logits,
    target_ids,
    lengths,
):
    positions, features = hidden_in.shape
    rows = positions // (chips * depth)
    xf = hidden_in.astype(jnp.float32)
    x_gained = (xf * pre_gain).astype(jnp.bfloat16)
    square_local = jnp.sum(xf * xf, axis=1)
    h_blocks, act, slope = ffn_forward(
        chips,
        x_gained,
        jnp.broadcast_to(square_local[:, None], (positions, 128)),
        gate_weight,
        up_weight,
    )
    hidden = h_blocks.reshape(positions, -1)
    x_blocks = hidden_in.reshape(chips, depth, rows, features)
    gains = jnp.pad(jnp.stack([post_gain, final_gain]), ((0, 6), (0, 0)))
    normed, y, side, teacher = branch_forward(
        chips, depth, hidden, down_weight, x_blocks, gains, teacher_logits
    )
    entries = embedding.shape[0]
    mask = token_mask(lengths, positions)
    count = jnp.sum(lengths).astype(jnp.float32)
    first_entry = lax.axis_index(("dp", "vocab")) * entries
    emb_blocks = embedding.reshape(entries, 2 * chips, features).transpose(1, 0, 2)
    stats, grad_emb, dy_blocks, back = head_both(
        chips,
        depth,
        normed.reshape(2 * chips, positions, features),
        emb_blocks,
        teacher.reshape(positions, entries),
        (loss_scale / count * mask)[:, None],
        (target_ids - first_entry)[:, None],
        y,
        side,
    )
    total_s, total_t, weighted, picked = stats[0], stats[1], stats[2], stats[3]
    log_s = jnp.log(total_s)
    log_t = jnp.log(total_t)
    per_token = weighted / total_t - log_t + log_s + hard_weight * (log_s - picked)
    loss = jnp.sum(mask * per_token) / count
    grad_embedding = grad_emb.transpose(1, 0, 2).reshape(entries, -1)
    grad_out = dy_blocks.reshape(positions, features)
    pairs = hidden_backward(chips, grad_out, down_weight, act, slope)
    dgate = pairs[:, :, 0].reshape(positions, -1)
    dup = pairs[:, :, 1].reshape(positions, -1)
    grad_down = contract_first(hidden, grad_out).astype(jnp.bfloat16)
    grad_gate = contract_first(x_gained, dgate).astype(jnp.bfloat16)
    grad_up = contract_first(x_gained, dup).astype(jnp.bfloat16)
    gain = jnp.broadcast_to(pre_gain[None, :], (8, features))
    grad_hidden = input_backward(
        chips, depth, dgate, dup, gate_weight, up_weight, x_blocks, gain, back
    ).reshape(positions, features)
    return (loss, grad_hidden, grad_gate, grad_up, grad_down, grad_embedding)


def pick_plan(mesh):
    chips = mesh.shape["dp"] // 2
    depth = mesh.shape["vocab"]
    tokens = LENGTH * 2
    if (
        mesh.shape["dp"] % 2 == 0
        and chips > 1
        and depth > 1
        and tokens % (32 * chips) == 0
        and tokens % (16 * chips * depth) == 0
    ):
        return functools.partial(on_device, chips, depth)
    return on_device_plain


def solution(mesh):
    return jax.shard_map(
        pick_plan(mesh),
        mesh=mesh,
        in_specs=(
            P(None, "dp"),
            P("dp"),
            P("dp", "vocab"),
            P("dp", "vocab"),
            P("vocab", "dp"),
            P("dp"),
            P("dp"),
            P(("dp", "vocab"), None),
            P("vocab", "dp"),
            P(),
            P(),
        ),
        out_specs=(
            P(),
            P(None, "dp"),
            P("dp", "vocab"),
            P("dp", "vocab"),
            P("vocab", "dp"),
            P(("dp", "vocab"), None),
        ),
        check_vma=False,
    )
```

```python
import functools
import jax
import jax.numpy as jnp
from jax import lax
from jax.experimental import pallas as pl
from jax.experimental.pallas import tpu as pltpu
from jax.sharding import PartitionSpec as P

D = 3584
LENGTH = 128


eps = 1e-06
softcap_value = 30.0
hard_weight = 0.5
loss_scale = 131072.0


def gelu_tanh(value):
    return jax.nn.gelu(value, approximate=True)


def token_mask(lengths, count):
    positions = jnp.arange(count, dtype=jnp.int32)
    sequence = positions // LENGTH
    within = positions % LENGTH
    match = sequence[:, None] == jnp.arange(lengths.shape[0], dtype=jnp.int32)[None, :]
    limit = jnp.sum(jnp.where(match, lengths[None, :], 0), axis=1)
    return jnp.where(within < limit, 1.0, 0.0).astype(jnp.float32)


def contract_last(left, right):
    return lax.dot_general(
        left, right, (((1,), (1,)), ((), ())), preferred_element_type=jnp.float32
    )


def contract_first(left, right):
    return lax.dot_general(
        left, right, (((0,), (0,)), ((), ())), preferred_element_type=jnp.float32
    )


def on_device_plain(
    hidden_in,
    pre_gain,
    gate_weight,
    up_weight,
    down_weight,
    post_gain,
    final_gain,
    embedding,
    teacher_logits,
    target_ids,
    lengths,
):
    positions = hidden_in.shape[0]
    xf = hidden_in.astype(jnp.float32)
    square_in = lax.psum(jnp.sum(xf * xf, axis=1), "dp")
    rms_in = lax.rsqrt(square_in / D + eps)[:, None]
    z = (xf * rms_in * pre_gain).astype(jnp.bfloat16)
    gate_terms = jnp.dot(z, gate_weight, preferred_element_type=jnp.float32)
    up_terms = jnp.dot(z, up_weight, preferred_element_type=jnp.float32)
    gate, up = lax.psum((gate_terms, up_terms), "dp")
    act, gelu_back = jax.vjp(gelu_tanh, gate)
    hidden = (act * up).astype(jnp.bfloat16)
    branch = lax.psum(jnp.dot(hidden, down_weight, preferred_element_type=jnp.float32), "vocab")
    gained = branch * post_gain
    square_br = lax.psum(jnp.sum(branch * branch, axis=1), "dp")
    rms_br = lax.rsqrt(square_br / D + eps)[:, None]
    stream = xf + gained * rms_br
    square_st = lax.psum(jnp.sum(stream * stream, axis=1), "dp")
    rms_st = lax.rsqrt(square_st / D + eps)[:, None]
    normed_local = (stream * rms_st * final_gain).astype(jnp.bfloat16)
    normed = lax.all_gather(normed_local, "dp", axis=1, tiled=True)
    raw = contract_last(normed, embedding)
    student = softcap_value * jnp.tanh(raw / softcap_value)
    teacher = lax.all_to_all(
        teacher_logits, "vocab", split_axis=1, concat_axis=0, tiled=True
    ).astype(jnp.float32)
    entries = embedding.shape[0]
    columns = lax.axis_index(("dp", "vocab")) * entries + jnp.arange(entries, dtype=jnp.int32)
    onehot = jnp.where(target_ids[:, None] == columns[None, :], 1.0, 0.0).astype(jnp.float32)
    exp_s = jnp.exp(student)
    exp_t = jnp.exp(teacher)
    total_s, total_t, weighted, picked = lax.psum(
        (
            jnp.sum(exp_s, axis=1),
            jnp.sum(exp_t, axis=1),
            jnp.sum(exp_t * (teacher - student), axis=1),
            jnp.sum(onehot * student, axis=1),
        ),
        ("dp", "vocab"),
    )
    log_s = jnp.log(total_s)
    log_t = jnp.log(total_t)
    mask = token_mask(lengths, positions)
    count = jnp.sum(lengths).astype(jnp.float32)
    per_token = weighted / total_t - log_t + log_s + hard_weight * (log_s - picked)
    loss = jnp.sum(mask * per_token) / count
    factor = loss_scale / count * mask[:, None]
    dstudent = factor * (
        (1.0 + hard_weight) * exp_s / total_s[:, None]
        - exp_t / total_t[:, None]
        - hard_weight * onehot
    )
    capped = student / softcap_value
    dlogit = (dstudent * (1.0 - capped * capped)).astype(jnp.bfloat16)
    grad_embedding = contract_first(dlogit, normed).astype(jnp.bfloat16)
    partial_grad = jnp.dot(dlogit, embedding, preferred_element_type=jnp.float32)
    local_grad = lax.psum_scatter(partial_grad, "dp", scatter_dimension=1, tiled=True)
    dnormed = lax.psum(local_grad, "vocab")
    along = dnormed * final_gain
    cube_st = rms_st * rms_st * rms_st
    cube_br = rms_br * rms_br * rms_br
    stream_along = lax.psum(jnp.sum(stream * along, axis=1), "dp")
    dstream = rms_st * along - stream * cube_st * (stream_along[:, None] / D)
    back = dstream * post_gain
    branch_back = lax.psum(jnp.sum(branch * back, axis=1), "dp")
    mean_br = branch_back[:, None] / D
    dbranch = rms_br * back - branch * cube_br * mean_br
    grad_out = dbranch.astype(jnp.bfloat16)
    grad_down = contract_first(hidden, grad_out).astype(jnp.bfloat16)
    dh_terms = contract_last(grad_out, down_weight)
    dh = lax.psum(dh_terms, "dp")
    dgate = gelu_back(dh * up)[0].astype(jnp.bfloat16)
    dup = (dh * act).astype(jnp.bfloat16)
    grad_gate = contract_first(z, dgate).astype(jnp.bfloat16)
    grad_up = contract_first(z, dup).astype(jnp.bfloat16)
    dz = lax.psum(contract_last(dgate, gate_weight) + contract_last(dup, up_weight), "vocab")
    scaled = dz * pre_gain
    input_inner = lax.psum(jnp.sum(xf * scaled, axis=1), "dp")
    cube_in = rms_in * rms_in * rms_in
    dinput = rms_in * scaled - xf * cube_in * (input_inner[:, None] / D)
    grad_hidden = (dstream + dinput).astype(jnp.bfloat16)
    return (loss, grad_hidden, grad_gate, grad_up, grad_down, grad_embedding)


MESH_ID = pl.DeviceIdType.MESH
CUBE = 0.044715
ROOT = 0.7978845608028654
PIECES = 4


def vmem():
    return pl.BlockSpec(memory_space=pltpu.VMEM)


def send(src, dst, sems, slot, peer):
    copy = pltpu.make_async_remote_copy(
        src_ref=src,
        dst_ref=dst,
        send_sem=sems.at[0, slot],
        recv_sem=sems.at[1, slot],
        device_id=peer,
        device_id_type=MESH_ID,
    )
    copy.start()
    return copy


def greet(peers):
    barrier = pltpu.get_barrier_semaphore()
    for peer in peers:
        pl.semaphore_signal(barrier, inc=1, device_id=peer, device_id_type=MESH_ID)
    pl.semaphore_wait(barrier, len(peers))


def places(chips):
    dp = lax.axis_index("dp")
    z = lax.axis_index("vocab")
    chip, core = dp // 2, dp % 2
    sibling = (chip * 2 + 1 - core, z)
    others = [(((chip + k) % chips) * 2 + core, z) for k in range(1, chips)]
    return chip, core, sibling, others


def scatter_start(chips, part, got_pair, sems, base):
    chip, core, sibling, others = places(chips)
    pair = {}
    for k in list(range(1, chips)) + [0]:
        there = (chip + k) % chips
        pair[k] = send(part.at[there, 1 - core], got_pair.at[there], sems, base + k, sibling)
    return pair


def scatter_chips(chips, pair, part, got_pair, out_chip, got_chip, sems, base):
    chip, core, sibling, others = places(chips)
    far = []
    for k in range(1, chips):
        there = (chip + k) % chips
        pair[k].wait_recv()
        total = part[there, core].astype(jnp.float32) + got_pair[there].astype(jnp.float32)
        out_chip[k - 1] = total.astype(out_chip.dtype)
        far.append(
            send(out_chip.at[k - 1], got_chip.at[k - 1], sems, base + chips + k, others[k - 1])
        )
    return far


def scatter_end(chips, pair, far, part, got_pair, got_chip):
    chip, core, sibling, others = places(chips)
    pair[0].wait_recv()
    for copy in far:
        copy.wait_recv()

    def take(rows):
        total = part[chip, core, rows].astype(jnp.float32) + got_pair[chip, rows].astype(
            jnp.float32
        )
        for k in range(1, chips):
            total += got_chip[k - 1, rows].astype(jnp.float32)
        return total

    return take


def gather_start(chips, out, cols, sems, base):
    chip, core, sibling, others = places(chips)
    mine = out.at[(chip, core) + cols]
    sent = [send(mine, mine, sems, base + k, others[k - 1]) for k in range(1, chips)]
    return sent, send(mine, mine, sems, base, sibling)


def gather_pass(chips, out, cols, sent, sems, base):
    chip, core, sibling, others = places(chips)
    passed = []
    for k in range(1, chips):
        sent[k - 1].wait_recv()
        block = out.at[((chip + chips - k) % chips, core) + cols]
        passed.append(send(block, block, sems, base + chips + k, sibling))
    return passed


def finish(copies):
    for copy in copies:
        copy.wait_send()


def ffn_kernel(
    chips, rows, x_ref, square_ref, gate_ref, up_ref,
    h_ref, act_ref, slope_ref,
    part, got_pair, out_chip, got_chip, sq, sq_pair, sq_out, sq_chip, sems,
):
    chip, core, sibling, others = places(chips)
    greet([sibling] + others)
    cut = part.shape[-1]
    pieces = part.shape[0]
    sq[...] = square_ref[...].reshape(sq.shape)
    top = 4 * chips * pieces
    pair_sq = scatter_start(chips, sq, sq_pair, sems, top)
    pairs = []
    for i in range(pieces):
        for which, weight in ((0, gate_ref), (1, up_ref)):
            terms = jnp.dot(
                x_ref[...], weight[:, pl.ds(i * cut, cut)], preferred_element_type=jnp.float32
            )
            part[i, :, :, pl.ds(which * rows, rows), :] = terms.astype(jnp.bfloat16).reshape(
                chips, 2, rows, cut
            )
        pairs.append(
            scatter_start(chips, part.at[i], got_pair.at[i], sems, 4 * chips * i)
        )
    far_sq = scatter_chips(chips, pair_sq, sq, sq_pair, sq_out, sq_chip, sems, top)
    fars = []
    for i in range(pieces):
        fars.append(
            scatter_chips(
                chips, pairs[i], part.at[i], got_pair.at[i], out_chip.at[i], got_chip.at[i],
                sems, 4 * chips * i,
            )
        )
    take_sq = scatter_end(chips, pair_sq, far_sq, sq, sq_pair, sq_chip)
    rms = lax.rsqrt(take_sq(pl.ds(0, rows))[:, :1] / D + eps)
    copies = list(pair_sq.values()) + far_sq
    gathers = []
    for i in range(pieces):
        cols = pl.ds(i * cut, cut)
        take = scatter_end(chips, pairs[i], fars[i], part.at[i], got_pair.at[i], got_chip.at[i])
        gate = take(pl.ds(0, rows)) * rms
        up = take(pl.ds(rows, rows)) * rms
        square = gate * gate
        bend = jnp.tanh(ROOT * (gate + CUBE * gate * square))
        half = 0.5 * (1.0 + bend)
        act = gate * half
        slope = half + 0.5 * gate * (1.0 - bend * bend) * (ROOT * (1.0 + 3.0 * CUBE * square))
        h_ref[chip, core, :, cols] = (act * up).astype(jnp.bfloat16)
        gathers.append(
            gather_start(chips, h_ref, (slice(None), cols), sems, 4 * chips * i + 2 * chips)
        )
        act_ref[:, cols] = act * rms
        slope_ref[:, cols] = up * slope * rms
        copies += list(pairs[i].values()) + fars[i]
    for i in range(pieces):
        cols = (slice(None), pl.ds(i * cut, cut))
        sent, near = gathers[i]
        passed = gather_pass(chips, h_ref, cols, sent, sems, 4 * chips * i + 2 * chips)
        for copy in [near] + passed:
            copy.wait_recv()
        copies += sent + [near] + passed
    finish(copies)


def ffn_forward(chips, x_gained, squares, gate_weight, up_weight):
    tokens = x_gained.shape[0]
    ff = gate_weight.shape[1]
    rows = tokens // (2 * chips)
    pieces = PIECES if ff % (128 * PIECES) == 0 else 1
    cut = ff // pieces
    b16, f32 = jnp.bfloat16, jnp.float32
    return pl.pallas_call(
        functools.partial(ffn_kernel, chips, rows),
        out_shape=(
            jax.ShapeDtypeStruct((chips, 2, rows, ff), b16),
            jax.ShapeDtypeStruct((rows, ff), f32),
            jax.ShapeDtypeStruct((rows, ff), f32),
        ),
        in_specs=[vmem()] * 4,
        out_specs=(vmem(),) * 3,
        scratch_shapes=[
            pltpu.VMEM((pieces, chips, 2, 2 * rows, cut), b16),
            pltpu.VMEM((pieces, chips, 2 * rows, cut), b16),
            pltpu.VMEM((pieces, chips - 1, 2 * rows, cut), b16),
            pltpu.VMEM((pieces, chips - 1, 2 * rows, cut), b16),
            pltpu.VMEM((chips, 2, rows, 128), f32),
            pltpu.VMEM((chips, rows, 128), f32),
            pltpu.VMEM((chips - 1, rows, 128), f32),
            pltpu.VMEM((chips - 1, rows, 128), f32),
            pltpu.SemaphoreType.DMA((2, 4 * chips * pieces + 2 * chips)),
        ],
        compiler_params=pltpu.CompilerParams(
            collective_id=1, has_side_effects=True, vmem_limit_bytes=48 * 2**20
        ),
    )(x_gained, squares, gate_weight, up_weight)


def hidden_kernel(
    chips, rows, dy_ref, down_ref, act_ref, slope_ref,
    pair_ref, part, got_pair, out_chip, got_chip, sems,
):
    chip, core, sibling, others = places(chips)
    greet([sibling] + others)
    cut = part.shape[-1]
    pieces = part.shape[0]
    pairs = []
    for i in range(pieces):
        terms = jnp.dot(
            dy_ref[...], down_ref[:, pl.ds(i * cut, cut)], preferred_element_type=jnp.float32
        )
        part[i] = terms.astype(jnp.bfloat16).reshape(chips, 2, rows, cut)
        pairs.append(
            scatter_start(chips, part.at[i], got_pair.at[i], sems, 4 * chips * i)
        )
    fars = []
    for i in range(pieces):
        fars.append(
            scatter_chips(
                chips, pairs[i], part.at[i], got_pair.at[i], out_chip.at[i], got_chip.at[i],
                sems, 4 * chips * i,
            )
        )
    copies = []
    gathers = []
    for i in range(pieces):
        cols = pl.ds(i * cut, cut)
        take = scatter_end(chips, pairs[i], fars[i], part.at[i], got_pair.at[i], got_chip.at[i])
        dh = take(pl.ds(0, rows))
        pair_ref[chip, core, 0, :, cols] = (dh * slope_ref[:, cols]).astype(jnp.bfloat16)
        pair_ref[chip, core, 1, :, cols] = (dh * act_ref[:, cols]).astype(jnp.bfloat16)
        gathers.append(
            gather_start(
                chips, pair_ref, (slice(None), slice(None), cols), sems, 4 * chips * i + 2 * chips
            )
        )
        copies += list(pairs[i].values()) + fars[i]
    for i in range(pieces):
        cols = (slice(None), slice(None), pl.ds(i * cut, cut))
        sent, near = gathers[i]
        passed = gather_pass(chips, pair_ref, cols, sent, sems, 4 * chips * i + 2 * chips)
        for copy in [near] + passed:
            copy.wait_recv()
        copies += sent + [near] + passed
    finish(copies)


def hidden_backward(chips, dy, down_weight, act, slope):
    tokens = dy.shape[0]
    ff = down_weight.shape[1]
    rows = tokens // (2 * chips)
    pieces = PIECES if ff % (128 * PIECES) == 0 else 1
    cut = ff // pieces
    b16 = jnp.bfloat16
    return pl.pallas_call(
        functools.partial(hidden_kernel, chips, rows),
        out_shape=jax.ShapeDtypeStruct((chips, 2, 2, rows, ff), b16),
        in_specs=[vmem()] * 4,
        out_specs=vmem(),
        scratch_shapes=[
            pltpu.VMEM((pieces, chips, 2, rows, cut), b16),
            pltpu.VMEM((pieces, chips, rows, cut), b16),
            pltpu.VMEM((pieces, chips - 1, rows, cut), b16),
            pltpu.VMEM((pieces, chips - 1, rows, cut), b16),
            pltpu.SemaphoreType.DMA((2, 4 * chips * pieces)),
        ],
        compiler_params=pltpu.CompilerParams(
            collective_id=2, has_side_effects=True, vmem_limit_bytes=48 * 2**20
        ),
    )(dy, down_weight, act, slope)


def spots(chips, depth):
    dp = lax.axis_index("dp")
    z = lax.axis_index("vocab")
    chip, core = dp // 2, dp % 2
    group = [(lax.rem(dp + k, 2 * chips), z) for k in range(1, 2 * chips)]
    line = [(dp, lax.rem(z + k, depth)) for k in range(1, depth)]
    others = [(lax.rem(chip + k, chips) * 2 + core, z) for k in range(1, chips)]
    sibling = (chip * 2 + 1 - core, z)
    return dp, z, chip, core, group, line, others, sibling


def feature_sum(value):
    return jnp.sum(jnp.sum(value, axis=0), axis=1, keepdims=True)


def norms(y, side, rows):
    x = side[:, 0:rows, :]
    post = side[:, rows : rows + 1, :]
    final = side[:, rows + 1 : rows + 2, :]
    rms_br = lax.rsqrt(feature_sum(y * y) / D + eps)[None]
    stream = x + y * rms_br * post
    rms_st = lax.rsqrt(feature_sum(stream * stream) / D + eps)[None]
    return stream, rms_br, rms_st, post, final


def branch_kernel(
    chips, depth, h_ref, down_ref, x_ref, gains_ref, teacher_ref,
    normed_ref, y_ref, side_ref, logits_ref,
    side, part, got, total, sems,
):
    dp, z, chip, core, group, line, others, sibling = spots(chips, depth)
    rows = x_ref.shape[2]
    count = 2 * chips
    half = chips
    greet(group + line)
    base = 0
    sent = []
    entries = logits_ref.shape[2]
    tea = []
    for k in range(1, depth):
        cols = pl.ds(pl.multiple_of(lax.rem(z + k, depth) * entries, 128), entries)
        tea.append(send(teacher_ref.at[:, cols], logits_ref.at[z], sems, base + k, line[k - 1]))
    base += depth
    for q in range(chips):
        side[q, 0:rows, :] = x_ref[q, z].astype(jnp.float32)
        side[q, rows : rows + 8, :] = gains_ref[...]
    early = []
    for k in range(1, count):
        there = lax.rem(dp + k, count) // 2
        early.append(send(side.at[there], side_ref.at[dp], sems, base + k, group[k - 1]))
    base += count
    side_ref[dp] = side[chip]
    own = pl.ds(pl.multiple_of(z * entries, 128), entries)
    logits_ref[z] = teacher_ref[:, own]
    terms = contract_last(h_ref[...], down_ref[...])
    part[...] = terms.reshape(part.shape)
    down = []
    for k in range(1, depth):
        there = lax.rem(z + k, depth)
        down.append(send(part.at[:, there], got.at[k - 1], sems, base + k, line[k - 1]))
    base += depth
    for copy in down:
        copy.wait_recv()
    summed = part[:, z]
    for k in range(1, depth):
        summed += got[k - 1]
    total[...] = summed
    across = []
    for k in range(1, count):
        there = lax.rem(dp + k, count) // 2
        across.append(send(total.at[there], y_ref.at[dp], sems, base + k, group[k - 1]))
    base += count
    y_ref[dp] = total[chip]
    for copy in early + across:
        copy.wait_recv()
    stream, rms_br, rms_st, post, final = norms(y_ref[...], side_ref[...], rows)
    normed_ref[:, chip, z] = (stream * rms_st * final).astype(jnp.bfloat16)
    mine = pl.ds(core * half, half)
    up = []
    for k in range(1, depth):
        block = normed_ref.at[mine, chip, z]
        up.append(send(block, block, sems, base + k, line[k - 1]))
    base += depth
    wide = []
    passed = []
    for k in range(depth):
        at = lax.rem(z + depth - k, depth)
        block = normed_ref.at[mine, chip, at]
        if k:
            up[k - 1].wait_recv()
            passed.append(send(block, block, sems, base + chips * depth + k, sibling))
        for j in range(1, chips):
            wide.append((j, send(block, block, sems, base + k * chips + j, others[j - 1])))
    base += chips * depth + depth
    for j in range(1, chips):
        for other, copy in wide:
            if other == j:
                copy.wait_recv()
        block = normed_ref.at[mine, lax.rem(chip + chips - j, chips)]
        passed.append(send(block, block, sems, base + j, sibling))
    for copy in passed + tea:
        copy.wait_recv()
    finish(tea + early + down + across + up + passed + [copy for _, copy in wide])


def branch_forward(chips, depth, hidden, down_weight, x_blocks, gains, teacher_logits):
    _, _, rows, features = x_blocks.shape
    entries = teacher_logits.shape[1] // depth
    count = 2 * chips
    f32 = jnp.float32
    return pl.pallas_call(
        functools.partial(branch_kernel, chips, depth),
        out_shape=(
            jax.ShapeDtypeStruct((count, chips, depth, rows, features), jnp.bfloat16),
            jax.ShapeDtypeStruct((count, rows, features), f32),
            jax.ShapeDtypeStruct((count, rows + 8, features), f32),
            jax.ShapeDtypeStruct((depth, teacher_logits.shape[0], entries), jnp.bfloat16),
        ),
        in_specs=[vmem()] * 5,
        out_specs=(vmem(),) * 4,
        scratch_shapes=[
            pltpu.VMEM((chips, rows + 8, features), f32),
            pltpu.VMEM((chips, depth, rows, features), f32),
            pltpu.VMEM((depth - 1, chips, rows, features), f32),
            pltpu.VMEM((chips, rows, features), f32),
            pltpu.SemaphoreType.DMA((2, 4 * depth + 5 * chips + chips * depth)),
        ],
        compiler_params=pltpu.CompilerParams(
            collective_id=3, has_side_effects=True, vmem_limit_bytes=48 * 2**20
        ),
    )(hidden, down_weight, x_blocks, gains, teacher_logits)


def head_kernel(
    chips, depth, normed_ref, emb_full, teacher_ref, factor_ref, local_ref, y_ref, side_ref,
    stats_ref, grad_emb_ref, dy_ref, back_ref,
    student, exp_s, exp_t, flat, near, dp_stats, z_stats,
    emb_ref, part, got_pair, out_chip, got_chip, line_part, got_line, owned, pay, sems,
):
    dp, z, chip, core, group, line, others, sibling = spots(chips, depth)
    count = 2 * chips
    half = chips
    rows = y_ref.shape[1]
    tokens, entries = teacher_ref.shape
    f32, b16 = jnp.float32, jnp.bfloat16
    greet(group + line)
    width = emb_full.shape[1] // count
    for d in range(count):
        emb_ref[d] = emb_full[:, d * width : (d + 1) * width]
    raw = contract_last(normed_ref[0], emb_ref[0])
    for d in range(1, count):
        raw += contract_last(normed_ref[d], emb_ref[d])
    logits = softcap_value * jnp.tanh(raw / softcap_value)
    student[...] = logits
    teacher = teacher_ref[...].astype(f32)
    exp_s[...] = jnp.exp(logits)
    exp_t[...] = jnp.exp(teacher)
    hot = local_ref[...] == lax.broadcasted_iota(jnp.int32, (tokens, entries), 1)
    lane = lax.broadcasted_iota(jnp.int32, (tokens, 128), 1)
    sums = [
        jnp.sum(exp_s[...], axis=1, keepdims=True),
        jnp.sum(exp_t[...], axis=1, keepdims=True),
        jnp.sum(exp_t[...] * (teacher - logits), axis=1, keepdims=True),
        jnp.sum(jnp.where(hot, logits, 0.0), axis=1, keepdims=True),
    ]
    columns = jnp.zeros((tokens, 128), f32)
    for i, value in enumerate(sums):
        columns = jnp.where(lane == i, value, columns)
    near[...] = columns.T[0:8, :]
    base = 0
    first = []
    for k in range(1, count):
        first.append(send(near, dp_stats.at[dp], sems, base + k, group[k - 1]))
    base += count
    dp_stats[dp] = near[...]
    for copy in first:
        copy.wait_recv()
    z_stats[z] = jnp.sum(dp_stats[...], axis=0)
    second = []
    for k in range(1, depth):
        second.append(send(z_stats.at[z], z_stats.at[z], sems, base + k, line[k - 1]))
    base += depth
    for copy in second:
        copy.wait_recv()
    whole = jnp.sum(z_stats[...], axis=0)
    stats_ref[...] = whole
    flat[...] = jnp.zeros_like(flat)
    flat[0:8, :] = whole
    columns = flat[...].T
    total_s = columns[:, 0:1]
    total_t = columns[:, 1:2]
    capped = student[...] / softcap_value
    dstudent = factor_ref[...] * (
        exp_s[...] * ((1.0 + hard_weight) / total_s)
        - exp_t[...] / total_t
        - jnp.where(hot, hard_weight, 0.0)
    )
    dlogit = (dstudent * (1.0 - capped * capped)).astype(b16)
    for d in range(count):
        terms = jnp.dot(dlogit, emb_ref[d], preferred_element_type=f32)
        part[d] = terms.astype(b16).reshape(chips, depth, rows, -1)
    theirs = pl.ds((1 - core) * half, half)
    mine = pl.ds(core * half, half)
    order = list(range(1, chips)) + [0]
    pair = {}
    for k in order:
        there = lax.rem(chip + k, chips)
        pair[k] = send(part.at[theirs, there], got_pair.at[:, there], sems, base + k, sibling)
    base += chips
    far = []
    for k in range(1, chips):
        there = lax.rem(chip + k, chips)
        pair[k].wait_recv()
        for i in range(half):
            out_chip[k - 1, i] = (
                part[core * half + i, there].astype(f32) + got_pair[i, there].astype(f32)
            ).astype(b16)
        far.append(send(out_chip.at[k - 1], got_chip.at[k - 1], sems, base + k, others[k - 1]))
    base += chips
    for d in range(0, count, 2):
        grad_emb_ref[:, d * width : (d + 2) * width] = jnp.concatenate(
            [contract_first(dlogit, normed_ref[d + i]) for i in range(2)], axis=1
        ).astype(b16)
    pair[0].wait_recv()
    for copy in far:
        copy.wait_recv()
    for i in range(half):
        value = part[core * half + i, chip].astype(f32) + got_pair[i, chip].astype(f32)
        for k in range(1, chips):
            value += got_chip[k - 1, i].astype(f32)
        line_part[:, i] = value.astype(b16)
    across = []
    for k in range(1, depth):
        there = lax.rem(z + k, depth)
        across.append(send(line_part.at[there], got_line.at[k - 1], sems, base + k, line[k - 1]))
    base += depth
    for copy in across:
        copy.wait_recv()
    value = line_part[z].astype(f32)
    for k in range(1, depth):
        value += got_line[k - 1].astype(f32)
    owned[mine] = value
    swap = send(owned.at[mine], owned.at[mine], sems, base, sibling)
    base += 1
    y = y_ref[...]
    stream, rms_br, rms_st, post, final = norms(y, side_ref[...], rows)
    swap.wait_recv()
    along = owned[...] * final
    mean_st = feature_sum(stream * along)[None] / D
    dstream = rms_st * along - stream * (rms_st * rms_st * rms_st) * mean_st
    back = dstream * post
    mean_br = feature_sum(y * back)[None] / D
    dbranch = rms_br * back - y * (rms_br * rms_br * rms_br) * mean_br
    pay[:, 0] = dbranch.astype(b16)
    pay[:, 1] = dstream.astype(b16)
    home = []
    for k in range(1, chips):
        there = lax.rem(chip + k, chips) * 2 + core
        home.append(send(pay.at[there], back_ref.at[chip], sems, base + k, others[k - 1]))
    base += chips
    back_ref[chip] = pay[dp]
    for copy in home:
        copy.wait_recv()
    dy_ref[:, z] = back_ref[:, 0]
    last = []
    for k in range(1, depth):
        last.append(send(dy_ref.at[:, z], dy_ref.at[:, z], sems, base + k, line[k - 1]))
    for copy in last:
        copy.wait_recv()
    finish(first + second + list(pair.values()) + far + across + [swap] + home + last)


def head_both(chips, depth, normed, embedding, teacher, factor, local, y, side):
    count, tokens, features = normed.shape
    entries = embedding.shape[0]
    rows = y.shape[1]
    f32, b16 = jnp.float32, jnp.bfloat16
    return pl.pallas_call(
        functools.partial(head_kernel, chips, depth),
        out_shape=(
            jax.ShapeDtypeStruct((8, tokens), f32),
            jax.ShapeDtypeStruct((entries, count * features), b16),
            jax.ShapeDtypeStruct((chips, depth, rows, features), b16),
            jax.ShapeDtypeStruct((chips, 2, rows, features), b16),
        ),
        in_specs=[vmem()] * 7,
        out_specs=(vmem(),) * 4,
        scratch_shapes=[
            pltpu.VMEM((tokens, entries), f32),
            pltpu.VMEM((tokens, entries), f32),
            pltpu.VMEM((tokens, entries), f32),
            pltpu.VMEM((128, tokens), f32),
            pltpu.VMEM((8, tokens), f32),
            pltpu.VMEM((count, 8, tokens), f32),
            pltpu.VMEM((depth, 8, tokens), f32),
            pltpu.VMEM((count, entries, features), b16),
            pltpu.VMEM((count, chips, depth, rows, features), b16),
            pltpu.VMEM((chips, chips, depth, rows, features), b16),
            pltpu.VMEM((chips - 1, chips, depth, rows, features), b16),
            pltpu.VMEM((chips - 1, chips, depth, rows, features), b16),
            pltpu.VMEM((depth, chips, rows, features), b16),
            pltpu.VMEM((depth - 1, chips, rows, features), b16),
            pltpu.VMEM((count, rows, features), f32),
            pltpu.VMEM((count, 2, rows, features), b16),
            pltpu.SemaphoreType.DMA((2, 5 * chips + 3 * depth + 1)),
        ],
        compiler_params=pltpu.CompilerParams(
            collective_id=4, has_side_effects=True, vmem_limit_bytes=48 * 2**20
        ),
    )(normed, embedding, teacher, factor, local, y, side)


def input_kernel(
    chips, depth, dgate_ref, dup_ref, gate_ref, up_ref, x_ref, gain_ref, back_ref,
    out_ref, part, got, scaled, mine, inner, sems,
):
    dp, z, chip, core, group, line, others, sibling = spots(chips, depth)
    count = 2 * chips
    f32, b16 = jnp.float32, jnp.bfloat16
    rows = x_ref.shape[2]
    greet(group + line)
    dz = contract_last(dgate_ref[...], gate_ref[...]) + contract_last(dup_ref[...], up_ref[...])
    part[...] = (dz * gain_ref[0:1, :]).astype(b16).reshape(part.shape)
    base = 0
    first = []
    for k in range(1, depth):
        there = lax.rem(z + k, depth)
        first.append(send(part.at[:, there], got.at[k - 1], sems, base + k, line[k - 1]))
    base += depth
    for copy in first:
        copy.wait_recv()
    value = part[:, z].astype(f32)
    for k in range(1, depth):
        value += got[k - 1].astype(f32)
    scaled[...] = value
    x = x_ref[:, z].astype(f32)
    lane = lax.broadcasted_iota(jnp.int32, (chips, rows, 128), 2)
    products = jnp.sum(x * value, axis=2, keepdims=True)
    squares = jnp.sum(x * x, axis=2, keepdims=True)
    mine[...] = jnp.where(lane == 0, products, jnp.where(lane == 1, squares, 0.0))
    second = []
    for k in range(1, count):
        second.append(send(mine, inner.at[dp], sems, base + k, group[k - 1]))
    base += count
    inner[dp] = mine[...]
    for copy in second:
        copy.wait_recv()
    sums = jnp.sum(inner[...], axis=0)
    mean = sums[:, :, 0:1] / D / (sums[:, :, 1:2] / D + eps)
    out_ref[:, z] = (back_ref[:, 1].astype(f32) + scaled[...] - x * mean).astype(b16)
    last = []
    for k in range(1, depth):
        last.append(send(out_ref.at[:, z], out_ref.at[:, z], sems, base + k, line[k - 1]))
    for copy in last:
        copy.wait_recv()
    finish(first + second + last)


def input_backward(chips, depth, dgate, dup, gate_weight, up_weight, x_blocks, gain, back):
    _, _, rows, features = x_blocks.shape
    f32, b16 = jnp.float32, jnp.bfloat16
    return pl.pallas_call(
        functools.partial(input_kernel, chips, depth),
        out_shape=jax.ShapeDtypeStruct((chips, depth, rows, features), b16),
        in_specs=[vmem()] * 7,
        out_specs=vmem(),
        scratch_shapes=[
            pltpu.VMEM((chips, depth, rows, features), b16),
            pltpu.VMEM((depth - 1, chips, rows, features), b16),
            pltpu.VMEM((chips, rows, features), f32),
            pltpu.VMEM((chips, rows, 128), f32),
            pltpu.VMEM((2 * chips, chips, rows, 128), f32),
            pltpu.SemaphoreType.DMA((2, 2 * depth + 2 * chips)),
        ],
        compiler_params=pltpu.CompilerParams(
            collective_id=5, has_side_effects=True, vmem_limit_bytes=48 * 2**20
        ),
    )(dgate, dup, gate_weight, up_weight, x_blocks, gain, back)


def on_device(
    chips,
    depth,
    hidden_in,
    pre_gain,
    gate_weight,
    up_weight,
    down_weight,
    post_gain,
    final_gain,
    embedding,
    teacher_logits,
    target_ids,
    lengths,
):
    positions, features = hidden_in.shape
    rows = positions // (chips * depth)
    xf = hidden_in.astype(jnp.float32)
    x_gained = (xf * pre_gain).astype(jnp.bfloat16)
    square_local = jnp.sum(xf * xf, axis=1)
    h_blocks, act, slope = ffn_forward(
        chips,
        x_gained,
        jnp.broadcast_to(square_local[:, None], (positions, 128)),
        gate_weight,
        up_weight,
    )
    hidden = h_blocks.reshape(positions, -1)
    x_blocks = hidden_in.reshape(chips, depth, rows, features)
    gains = jnp.pad(jnp.stack([post_gain, final_gain]), ((0, 6), (0, 0)))
    normed, y, side, teacher = branch_forward(
        chips, depth, hidden, down_weight.T, x_blocks, gains, teacher_logits
    )
    entries = embedding.shape[0]
    mask = token_mask(lengths, positions)
    count = jnp.sum(lengths).astype(jnp.float32)
    first_entry = lax.axis_index(("dp", "vocab")) * entries
    stats, grad_emb, dy_blocks, back = head_both(
        chips,
        depth,
        normed.reshape(2 * chips, positions, features),
        embedding,
        teacher.reshape(positions, entries),
        (loss_scale / count * mask)[:, None],
        (target_ids - first_entry)[:, None],
        y,
        side,
    )
    total_s, total_t, weighted, picked = stats[0], stats[1], stats[2], stats[3]
    log_s = jnp.log(total_s)
    log_t = jnp.log(total_t)
    per_token = weighted / total_t - log_t + log_s + hard_weight * (log_s - picked)
    loss = jnp.sum(mask * per_token) / count
    grad_embedding = grad_emb
    grad_out = dy_blocks.reshape(positions, features)
    pairs = hidden_backward(chips, grad_out, down_weight.T, act, slope)
    dgate = pairs[:, :, 0].reshape(positions, -1)
    dup = pairs[:, :, 1].reshape(positions, -1)
    grad_down = contract_first(hidden, grad_out).astype(jnp.bfloat16)
    grad_gate = contract_first(x_gained, dgate).astype(jnp.bfloat16)
    grad_up = contract_first(x_gained, dup).astype(jnp.bfloat16)
    gain = jnp.broadcast_to(pre_gain[None, :], (8, features))
    grad_hidden = input_backward(
        chips, depth, dgate, dup, gate_weight, up_weight, x_blocks, gain, back
    ).reshape(positions, features)
    return (loss, grad_hidden, grad_gate, grad_up, grad_down, grad_embedding)


def pick_plan(mesh):
    chips = mesh.shape["dp"] // 2
    depth = mesh.shape["vocab"]
    tokens = LENGTH * 2
    if (
        mesh.shape["dp"] % 2 == 0
        and chips > 1
        and depth > 1
        and tokens % (32 * chips) == 0
        and tokens % (16 * chips * depth) == 0
    ):
        return functools.partial(on_device, chips, depth)
    return on_device_plain


def solution(mesh):
    return jax.shard_map(
        pick_plan(mesh),
        mesh=mesh,
        in_specs=(
            P(None, "dp"),
            P("dp"),
            P("dp", "vocab"),
            P("dp", "vocab"),
            P("vocab", "dp"),
            P("dp"),
            P("dp"),
            P(("dp", "vocab"), None),
            P("vocab", "dp"),
            P(),
            P(),
        ),
        out_specs=(
            P(),
            P(None, "dp"),
            P("dp", "vocab"),
            P("dp", "vocab"),
            P("vocab", "dp"),
            P(("dp", "vocab"), None),
        ),
        check_vma=False,
    )
```

```python
import functools
import jax
import jax.numpy as jnp
from jax import lax
from jax.experimental import pallas as pl
from jax.experimental.pallas import tpu as pltpu
from jax.sharding import PartitionSpec as P

D = 3584
LENGTH = 128


eps = 1e-06
softcap_value = 30.0
hard_weight = 0.5
loss_scale = 131072.0


def gelu_tanh(value):
    return jax.nn.gelu(value, approximate=True)


def token_mask(lengths, count):
    positions = jnp.arange(count, dtype=jnp.int32)
    sequence = positions // LENGTH
    within = positions % LENGTH
    match = sequence[:, None] == jnp.arange(lengths.shape[0], dtype=jnp.int32)[None, :]
    limit = jnp.sum(jnp.where(match, lengths[None, :], 0), axis=1)
    return jnp.where(within < limit, 1.0, 0.0).astype(jnp.float32)


def contract_last(left, right):
    return lax.dot_general(
        left, right, (((1,), (1,)), ((), ())), preferred_element_type=jnp.float32
    )


def contract_first(left, right):
    return lax.dot_general(
        left, right, (((0,), (0,)), ((), ())), preferred_element_type=jnp.float32
    )


def on_device_plain(
    hidden_in,
    pre_gain,
    gate_weight,
    up_weight,
    down_weight,
    post_gain,
    final_gain,
    embedding,
    teacher_logits,
    target_ids,
    lengths,
):
    positions = hidden_in.shape[0]
    xf = hidden_in.astype(jnp.float32)
    square_in = lax.psum(jnp.sum(xf * xf, axis=1), "dp")
    rms_in = lax.rsqrt(square_in / D + eps)[:, None]
    z = (xf * rms_in * pre_gain).astype(jnp.bfloat16)
    gate_terms = jnp.dot(z, gate_weight, preferred_element_type=jnp.float32)
    up_terms = jnp.dot(z, up_weight, preferred_element_type=jnp.float32)
    gate, up = lax.psum((gate_terms, up_terms), "dp")
    act, gelu_back = jax.vjp(gelu_tanh, gate)
    hidden = (act * up).astype(jnp.bfloat16)
    branch = lax.psum(jnp.dot(hidden, down_weight, preferred_element_type=jnp.float32), "vocab")
    gained = branch * post_gain
    square_br = lax.psum(jnp.sum(branch * branch, axis=1), "dp")
    rms_br = lax.rsqrt(square_br / D + eps)[:, None]
    stream = xf + gained * rms_br
    square_st = lax.psum(jnp.sum(stream * stream, axis=1), "dp")
    rms_st = lax.rsqrt(square_st / D + eps)[:, None]
    normed_local = (stream * rms_st * final_gain).astype(jnp.bfloat16)
    normed = lax.all_gather(normed_local, "dp", axis=1, tiled=True)
    raw = contract_last(normed, embedding)
    student = softcap_value * jnp.tanh(raw / softcap_value)
    teacher = lax.all_to_all(
        teacher_logits, "vocab", split_axis=1, concat_axis=0, tiled=True
    ).astype(jnp.float32)
    entries = embedding.shape[0]
    columns = lax.axis_index(("dp", "vocab")) * entries + jnp.arange(entries, dtype=jnp.int32)
    onehot = jnp.where(target_ids[:, None] == columns[None, :], 1.0, 0.0).astype(jnp.float32)
    exp_s = jnp.exp(student)
    exp_t = jnp.exp(teacher)
    total_s, total_t, weighted, picked = lax.psum(
        (
            jnp.sum(exp_s, axis=1),
            jnp.sum(exp_t, axis=1),
            jnp.sum(exp_t * (teacher - student), axis=1),
            jnp.sum(onehot * student, axis=1),
        ),
        ("dp", "vocab"),
    )
    log_s = jnp.log(total_s)
    log_t = jnp.log(total_t)
    mask = token_mask(lengths, positions)
    count = jnp.sum(lengths).astype(jnp.float32)
    per_token = weighted / total_t - log_t + log_s + hard_weight * (log_s - picked)
    loss = jnp.sum(mask * per_token) / count
    factor = loss_scale / count * mask[:, None]
    dstudent = factor * (
        (1.0 + hard_weight) * exp_s / total_s[:, None]
        - exp_t / total_t[:, None]
        - hard_weight * onehot
    )
    capped = student / softcap_value
    dlogit = (dstudent * (1.0 - capped * capped)).astype(jnp.bfloat16)
    grad_embedding = contract_first(dlogit, normed).astype(jnp.bfloat16)
    partial_grad = jnp.dot(dlogit, embedding, preferred_element_type=jnp.float32)
    local_grad = lax.psum_scatter(partial_grad, "dp", scatter_dimension=1, tiled=True)
    dnormed = lax.psum(local_grad, "vocab")
    along = dnormed * final_gain
    cube_st = rms_st * rms_st * rms_st
    cube_br = rms_br * rms_br * rms_br
    stream_along = lax.psum(jnp.sum(stream * along, axis=1), "dp")
    dstream = rms_st * along - stream * cube_st * (stream_along[:, None] / D)
    back = dstream * post_gain
    branch_back = lax.psum(jnp.sum(branch * back, axis=1), "dp")
    mean_br = branch_back[:, None] / D
    dbranch = rms_br * back - branch * cube_br * mean_br
    grad_out = dbranch.astype(jnp.bfloat16)
    grad_down = contract_first(hidden, grad_out).astype(jnp.bfloat16)
    dh_terms = contract_last(grad_out, down_weight)
    dh = lax.psum(dh_terms, "dp")
    dgate = gelu_back(dh * up)[0].astype(jnp.bfloat16)
    dup = (dh * act).astype(jnp.bfloat16)
    grad_gate = contract_first(z, dgate).astype(jnp.bfloat16)
    grad_up = contract_first(z, dup).astype(jnp.bfloat16)
    dz = lax.psum(contract_last(dgate, gate_weight) + contract_last(dup, up_weight), "vocab")
    scaled = dz * pre_gain
    input_inner = lax.psum(jnp.sum(xf * scaled, axis=1), "dp")
    cube_in = rms_in * rms_in * rms_in
    dinput = rms_in * scaled - xf * cube_in * (input_inner[:, None] / D)
    grad_hidden = (dstream + dinput).astype(jnp.bfloat16)
    return (loss, grad_hidden, grad_gate, grad_up, grad_down, grad_embedding)


MESH_ID = pl.DeviceIdType.MESH
CUBE = 0.044715
ROOT = 0.7978845608028654
PIECES = 4


def vmem():
    return pl.BlockSpec(memory_space=pltpu.VMEM)


def send(src, dst, sems, slot, peer):
    copy = pltpu.make_async_remote_copy(
        src_ref=src,
        dst_ref=dst,
        send_sem=sems.at[0, slot],
        recv_sem=sems.at[1, slot],
        device_id=peer,
        device_id_type=MESH_ID,
    )
    copy.start()
    return copy


def greet(peers):
    barrier = pltpu.get_barrier_semaphore()
    for peer in peers:
        pl.semaphore_signal(barrier, inc=1, device_id=peer, device_id_type=MESH_ID)
    pl.semaphore_wait(barrier, len(peers))


def places(chips):
    dp = lax.axis_index("dp")
    z = lax.axis_index("vocab")
    chip, core = dp // 2, dp % 2
    sibling = (chip * 2 + 1 - core, z)
    others = [(((chip + k) % chips) * 2 + core, z) for k in range(1, chips)]
    return chip, core, sibling, others


def scatter_start(chips, part, got_pair, sems, base):
    chip, core, sibling, others = places(chips)
    pair = {}
    for k in list(range(1, chips)) + [0]:
        there = (chip + k) % chips
        pair[k] = send(part.at[there, 1 - core], got_pair.at[there], sems, base + k, sibling)
    return pair


def scatter_chips(chips, pair, part, got_pair, out_chip, got_chip, sems, base):
    chip, core, sibling, others = places(chips)
    far = []
    for k in range(1, chips):
        there = (chip + k) % chips
        pair[k].wait_recv()
        total = part[there, core].astype(jnp.float32) + got_pair[there].astype(jnp.float32)
        out_chip[k - 1] = total.astype(out_chip.dtype)
        far.append(
            send(out_chip.at[k - 1], got_chip.at[k - 1], sems, base + chips + k, others[k - 1])
        )
    return far


def scatter_end(chips, pair, far, part, got_pair, got_chip):
    chip, core, sibling, others = places(chips)
    pair[0].wait_recv()
    for copy in far:
        copy.wait_recv()

    def take(rows):
        total = part[chip, core, rows].astype(jnp.float32) + got_pair[chip, rows].astype(
            jnp.float32
        )
        for k in range(1, chips):
            total += got_chip[k - 1, rows].astype(jnp.float32)
        return total

    return take


def gather_start(chips, out, cols, sems, base):
    chip, core, sibling, others = places(chips)
    mine = out.at[(chip, core) + cols]
    sent = [send(mine, mine, sems, base + k, others[k - 1]) for k in range(1, chips)]
    return sent, send(mine, mine, sems, base, sibling)


def gather_pass(chips, out, cols, sent, sems, base):
    chip, core, sibling, others = places(chips)
    passed = []
    for k in range(1, chips):
        sent[k - 1].wait_recv()
        block = out.at[((chip + chips - k) % chips, core) + cols]
        passed.append(send(block, block, sems, base + chips + k, sibling))
    return passed


def finish(copies):
    for copy in copies:
        copy.wait_send()


def ffn_kernel(
    chips, rows, x_ref, square_ref, gate_ref, up_ref,
    h_ref, act_ref, slope_ref,
    part, got_pair, out_chip, got_chip, sq, sq_pair, sq_out, sq_chip, sems,
):
    chip, core, sibling, others = places(chips)
    greet([sibling] + others)
    cut = part.shape[-1]
    pieces = part.shape[0]
    sq[...] = square_ref[...].reshape(sq.shape)
    top = 4 * chips * pieces
    pair_sq = scatter_start(chips, sq, sq_pair, sems, top)
    pairs = []
    for i in range(pieces):
        for which, weight in ((0, gate_ref), (1, up_ref)):
            terms = jnp.dot(
                x_ref[...], weight[:, pl.ds(i * cut, cut)], preferred_element_type=jnp.float32
            )
            part[i, :, :, pl.ds(which * rows, rows), :] = terms.astype(jnp.bfloat16).reshape(
                chips, 2, rows, cut
            )
        pairs.append(
            scatter_start(chips, part.at[i], got_pair.at[i], sems, 4 * chips * i)
        )
    far_sq = scatter_chips(chips, pair_sq, sq, sq_pair, sq_out, sq_chip, sems, top)
    fars = []
    for i in range(pieces):
        fars.append(
            scatter_chips(
                chips, pairs[i], part.at[i], got_pair.at[i], out_chip.at[i], got_chip.at[i],
                sems, 4 * chips * i,
            )
        )
    take_sq = scatter_end(chips, pair_sq, far_sq, sq, sq_pair, sq_chip)
    rms = lax.rsqrt(take_sq(pl.ds(0, rows))[:, :1] / D + eps)
    copies = list(pair_sq.values()) + far_sq
    gathers = []
    for i in range(pieces):
        cols = pl.ds(i * cut, cut)
        take = scatter_end(chips, pairs[i], fars[i], part.at[i], got_pair.at[i], got_chip.at[i])
        gate = take(pl.ds(0, rows)) * rms
        up = take(pl.ds(rows, rows)) * rms
        square = gate * gate
        bend = jnp.tanh(ROOT * (gate + CUBE * gate * square))
        half = 0.5 * (1.0 + bend)
        act = gate * half
        slope = half + 0.5 * gate * (1.0 - bend * bend) * (ROOT * (1.0 + 3.0 * CUBE * square))
        h_ref[chip, core, :, cols] = (act * up).astype(jnp.bfloat16)
        gathers.append(
            gather_start(chips, h_ref, (slice(None), cols), sems, 4 * chips * i + 2 * chips)
        )
        act_ref[:, cols] = act * rms
        slope_ref[:, cols] = up * slope * rms
        copies += list(pairs[i].values()) + fars[i]
    for i in range(pieces):
        cols = (slice(None), pl.ds(i * cut, cut))
        sent, near = gathers[i]
        passed = gather_pass(chips, h_ref, cols, sent, sems, 4 * chips * i + 2 * chips)
        for copy in [near] + passed:
            copy.wait_recv()
        copies += sent + [near] + passed
    finish(copies)


def ffn_forward(chips, x_gained, squares, gate_weight, up_weight):
    tokens = x_gained.shape[0]
    ff = gate_weight.shape[1]
    rows = tokens // (2 * chips)
    pieces = PIECES if ff % (128 * PIECES) == 0 else 1
    cut = ff // pieces
    b16, f32 = jnp.bfloat16, jnp.float32
    return pl.pallas_call(
        functools.partial(ffn_kernel, chips, rows),
        out_shape=(
            jax.ShapeDtypeStruct((chips, 2, rows, ff), b16),
            jax.ShapeDtypeStruct((rows, ff), f32),
            jax.ShapeDtypeStruct((rows, ff), f32),
        ),
        in_specs=[vmem()] * 4,
        out_specs=(vmem(),) * 3,
        scratch_shapes=[
            pltpu.VMEM((pieces, chips, 2, 2 * rows, cut), b16),
            pltpu.VMEM((pieces, chips, 2 * rows, cut), b16),
            pltpu.VMEM((pieces, chips - 1, 2 * rows, cut), b16),
            pltpu.VMEM((pieces, chips - 1, 2 * rows, cut), b16),
            pltpu.VMEM((chips, 2, rows, 128), f32),
            pltpu.VMEM((chips, rows, 128), f32),
            pltpu.VMEM((chips - 1, rows, 128), f32),
            pltpu.VMEM((chips - 1, rows, 128), f32),
            pltpu.SemaphoreType.DMA((2, 4 * chips * pieces + 2 * chips)),
        ],
        compiler_params=pltpu.CompilerParams(
            collective_id=1, has_side_effects=True, vmem_limit_bytes=48 * 2**20
        ),
    )(x_gained, squares, gate_weight, up_weight)


def hidden_kernel(
    chips, rows, dy_ref, down_ref, act_ref, slope_ref,
    pair_ref, part, got_pair, out_chip, got_chip, sems,
):
    chip, core, sibling, others = places(chips)
    greet([sibling] + others)
    cut = part.shape[-1]
    pieces = part.shape[0]
    pairs = []
    for i in range(pieces):
        terms = jnp.dot(
            dy_ref[...], down_ref[:, pl.ds(i * cut, cut)], preferred_element_type=jnp.float32
        )
        part[i] = terms.astype(jnp.bfloat16).reshape(chips, 2, rows, cut)
        pairs.append(
            scatter_start(chips, part.at[i], got_pair.at[i], sems, 4 * chips * i)
        )
    fars = []
    for i in range(pieces):
        fars.append(
            scatter_chips(
                chips, pairs[i], part.at[i], got_pair.at[i], out_chip.at[i], got_chip.at[i],
                sems, 4 * chips * i,
            )
        )
    copies = []
    gathers = []
    for i in range(pieces):
        cols = pl.ds(i * cut, cut)
        take = scatter_end(chips, pairs[i], fars[i], part.at[i], got_pair.at[i], got_chip.at[i])
        dh = take(pl.ds(0, rows))
        pair_ref[chip, core, 0, :, cols] = (dh * slope_ref[:, cols]).astype(jnp.bfloat16)
        pair_ref[chip, core, 1, :, cols] = (dh * act_ref[:, cols]).astype(jnp.bfloat16)
        gathers.append(
            gather_start(
                chips, pair_ref, (slice(None), slice(None), cols), sems, 4 * chips * i + 2 * chips
            )
        )
        copies += list(pairs[i].values()) + fars[i]
    for i in range(pieces):
        cols = (slice(None), slice(None), pl.ds(i * cut, cut))
        sent, near = gathers[i]
        passed = gather_pass(chips, pair_ref, cols, sent, sems, 4 * chips * i + 2 * chips)
        for copy in [near] + passed:
            copy.wait_recv()
        copies += sent + [near] + passed
    finish(copies)


def hidden_backward(chips, dy, down_weight, act, slope):
    tokens = dy.shape[0]
    ff = down_weight.shape[1]
    rows = tokens // (2 * chips)
    pieces = PIECES if ff % (128 * PIECES) == 0 else 1
    cut = ff // pieces
    b16 = jnp.bfloat16
    return pl.pallas_call(
        functools.partial(hidden_kernel, chips, rows),
        out_shape=jax.ShapeDtypeStruct((chips, 2, 2, rows, ff), b16),
        in_specs=[vmem()] * 4,
        out_specs=vmem(),
        scratch_shapes=[
            pltpu.VMEM((pieces, chips, 2, rows, cut), b16),
            pltpu.VMEM((pieces, chips, rows, cut), b16),
            pltpu.VMEM((pieces, chips - 1, rows, cut), b16),
            pltpu.VMEM((pieces, chips - 1, rows, cut), b16),
            pltpu.SemaphoreType.DMA((2, 4 * chips * pieces)),
        ],
        compiler_params=pltpu.CompilerParams(
            collective_id=2, has_side_effects=True, vmem_limit_bytes=48 * 2**20
        ),
    )(dy, down_weight, act, slope)


def spots(chips, depth):
    dp = lax.axis_index("dp")
    z = lax.axis_index("vocab")
    chip, core = dp // 2, dp % 2
    group = [(lax.rem(dp + k, 2 * chips), z) for k in range(1, 2 * chips)]
    line = [(dp, lax.rem(z + k, depth)) for k in range(1, depth)]
    others = [(lax.rem(chip + k, chips) * 2 + core, z) for k in range(1, chips)]
    sibling = (chip * 2 + 1 - core, z)
    return dp, z, chip, core, group, line, others, sibling


def feature_sum(value):
    return jnp.sum(jnp.sum(value, axis=0), axis=1, keepdims=True)


def norms(y, side, rows):
    x = side[:, 0:rows, :]
    post = side[:, rows : rows + 1, :]
    final = side[:, rows + 1 : rows + 2, :]
    rms_br = lax.rsqrt(feature_sum(y * y) / D + eps)[None]
    stream = x + y * rms_br * post
    rms_st = lax.rsqrt(feature_sum(stream * stream) / D + eps)[None]
    return stream, rms_br, rms_st, post, final


def branch_kernel(
    chips, depth, h_ref, down_ref, x_ref, gains_ref, teacher_ref,
    normed_ref, y_ref, side_ref, logits_ref,
    side, part, got, total, sems,
):
    dp, z, chip, core, group, line, others, sibling = spots(chips, depth)
    rows = x_ref.shape[2]
    count = 2 * chips
    half = chips
    greet(group + line)
    base = 0
    sent = []
    entries = logits_ref.shape[2]
    tea = []
    for k in range(1, depth):
        cols = pl.ds(pl.multiple_of(lax.rem(z + k, depth) * entries, 128), entries)
        tea.append(send(teacher_ref.at[:, cols], logits_ref.at[z], sems, base + k, line[k - 1]))
    base += depth
    for q in range(chips):
        side[q, 0:rows, :] = x_ref[q, z].astype(jnp.float32)
        side[q, rows : rows + 8, :] = gains_ref[...]
    early = []
    for k in range(1, count):
        there = lax.rem(dp + k, count) // 2
        early.append(send(side.at[there], side_ref.at[dp], sems, base + k, group[k - 1]))
    base += count
    side_ref[dp] = side[chip]
    own = pl.ds(pl.multiple_of(z * entries, 128), entries)
    logits_ref[z] = teacher_ref[:, own]
    terms = contract_last(h_ref[...], down_ref[...])
    part[...] = terms.astype(jnp.bfloat16).reshape(part.shape)
    down = []
    for k in range(1, depth):
        there = lax.rem(z + k, depth)
        down.append(send(part.at[:, there], got.at[k - 1], sems, base + k, line[k - 1]))
    base += depth
    for copy in down:
        copy.wait_recv()
    summed = part[:, z].astype(jnp.float32)
    for k in range(1, depth):
        summed += got[k - 1].astype(jnp.float32)
    total[...] = summed
    across = []
    for k in range(1, count):
        there = lax.rem(dp + k, count) // 2
        across.append(send(total.at[there], y_ref.at[dp], sems, base + k, group[k - 1]))
    base += count
    y_ref[dp] = total[chip]
    for copy in early + across:
        copy.wait_recv()
    stream, rms_br, rms_st, post, final = norms(y_ref[...], side_ref[...], rows)
    normed_ref[:, chip, z] = (stream * rms_st * final).astype(jnp.bfloat16)
    mine = pl.ds(core * half, half)
    up = []
    for k in range(1, depth):
        block = normed_ref.at[mine, chip, z]
        up.append(send(block, block, sems, base + k, line[k - 1]))
    base += depth
    wide = []
    passed = []
    for k in range(depth):
        at = lax.rem(z + depth - k, depth)
        block = normed_ref.at[mine, chip, at]
        if k:
            up[k - 1].wait_recv()
            passed.append(send(block, block, sems, base + chips * depth + k, sibling))
        for j in range(1, chips):
            wide.append((j, send(block, block, sems, base + k * chips + j, others[j - 1])))
    base += chips * depth + depth
    for j in range(1, chips):
        for other, copy in wide:
            if other == j:
                copy.wait_recv()
        block = normed_ref.at[mine, lax.rem(chip + chips - j, chips)]
        passed.append(send(block, block, sems, base + j, sibling))
    for copy in passed + tea:
        copy.wait_recv()
    finish(tea + early + down + across + up + passed + [copy for _, copy in wide])


def branch_forward(chips, depth, hidden, down_weight, x_blocks, gains, teacher_logits):
    _, _, rows, features = x_blocks.shape
    entries = teacher_logits.shape[1] // depth
    count = 2 * chips
    f32 = jnp.float32
    return pl.pallas_call(
        functools.partial(branch_kernel, chips, depth),
        out_shape=(
            jax.ShapeDtypeStruct((count, chips, depth, rows, features), jnp.bfloat16),
            jax.ShapeDtypeStruct((count, rows, features), f32),
            jax.ShapeDtypeStruct((count, rows + 8, features), f32),
            jax.ShapeDtypeStruct((depth, teacher_logits.shape[0], entries), jnp.bfloat16),
        ),
        in_specs=[vmem()] * 5,
        out_specs=(vmem(),) * 4,
        scratch_shapes=[
            pltpu.VMEM((chips, rows + 8, features), f32),
            pltpu.VMEM((chips, depth, rows, features), jnp.bfloat16),
            pltpu.VMEM((depth - 1, chips, rows, features), jnp.bfloat16),
            pltpu.VMEM((chips, rows, features), f32),
            pltpu.SemaphoreType.DMA((2, 4 * depth + 5 * chips + chips * depth)),
        ],
        compiler_params=pltpu.CompilerParams(
            collective_id=3, has_side_effects=True, vmem_limit_bytes=48 * 2**20
        ),
    )(hidden, down_weight, x_blocks, gains, teacher_logits)


def head_kernel(
    chips, depth, normed_ref, emb_full, teacher_ref, factor_ref, local_ref, y_ref, side_ref,
    stats_ref, grad_emb_ref, dy_ref, back_ref,
    student, exp_s, exp_t, flat, near, dp_stats, z_stats,
    emb_ref, part, got_pair, out_chip, got_chip, line_part, got_line, owned, pay, sems,
):
    dp, z, chip, core, group, line, others, sibling = spots(chips, depth)
    count = 2 * chips
    half = chips
    rows = y_ref.shape[1]
    tokens, entries = teacher_ref.shape
    f32, b16 = jnp.float32, jnp.bfloat16
    greet(group + line)
    width = emb_full.shape[1] // count
    for d in range(count):
        emb_ref[d] = emb_full[:, d * width : (d + 1) * width]
    raw = contract_last(normed_ref[0], emb_ref[0])
    for d in range(1, count):
        raw += contract_last(normed_ref[d], emb_ref[d])
    logits = softcap_value * jnp.tanh(raw / softcap_value)
    student[...] = logits
    teacher = teacher_ref[...].astype(f32)
    exp_s[...] = jnp.exp(logits)
    exp_t[...] = jnp.exp(teacher)
    hot = local_ref[...] == lax.broadcasted_iota(jnp.int32, (tokens, entries), 1)
    lane = lax.broadcasted_iota(jnp.int32, (tokens, 128), 1)
    sums = [
        jnp.sum(exp_s[...], axis=1, keepdims=True),
        jnp.sum(exp_t[...], axis=1, keepdims=True),
        jnp.sum(exp_t[...] * (teacher - logits), axis=1, keepdims=True),
        jnp.sum(jnp.where(hot, logits, 0.0), axis=1, keepdims=True),
    ]
    columns = jnp.zeros((tokens, 128), f32)
    for i, value in enumerate(sums):
        columns = jnp.where(lane == i, value, columns)
    near[...] = columns.T[0:8, :]
    base = 0
    first = []
    for k in range(1, count):
        first.append(send(near, dp_stats.at[dp], sems, base + k, group[k - 1]))
    base += count
    dp_stats[dp] = near[...]
    for copy in first:
        copy.wait_recv()
    z_stats[z] = jnp.sum(dp_stats[...], axis=0)
    second = []
    for k in range(1, depth):
        second.append(send(z_stats.at[z], z_stats.at[z], sems, base + k, line[k - 1]))
    base += depth
    for copy in second:
        copy.wait_recv()
    whole = jnp.sum(z_stats[...], axis=0)
    stats_ref[...] = whole
    flat[...] = jnp.zeros_like(flat)
    flat[0:8, :] = whole
    columns = flat[...].T
    total_s = columns[:, 0:1]
    total_t = columns[:, 1:2]
    capped = student[...] / softcap_value
    dstudent = factor_ref[...] * (
        exp_s[...] * ((1.0 + hard_weight) / total_s)
        - exp_t[...] / total_t
        - jnp.where(hot, hard_weight, 0.0)
    )
    dlogit = (dstudent * (1.0 - capped * capped)).astype(b16)
    for d in range(count):
        terms = jnp.dot(dlogit, emb_ref[d], preferred_element_type=f32)
        part[d] = terms.astype(b16).reshape(chips, depth, rows, -1)
    theirs = pl.ds((1 - core) * half, half)
    mine = pl.ds(core * half, half)
    order = list(range(1, chips)) + [0]
    pair = {}
    for k in order:
        there = lax.rem(chip + k, chips)
        pair[k] = send(part.at[theirs, there], got_pair.at[:, there], sems, base + k, sibling)
    base += chips
    far = []
    for k in range(1, chips):
        there = lax.rem(chip + k, chips)
        pair[k].wait_recv()
        for i in range(half):
            out_chip[k - 1, i] = (
                part[core * half + i, there].astype(f32) + got_pair[i, there].astype(f32)
            ).astype(b16)
        far.append(send(out_chip.at[k - 1], got_chip.at[k - 1], sems, base + k, others[k - 1]))
    base += chips
    for d in range(0, count, 2):
        grad_emb_ref[:, d * width : (d + 2) * width] = jnp.concatenate(
            [contract_first(dlogit, normed_ref[d + i]) for i in range(2)], axis=1
        ).astype(b16)
    pair[0].wait_recv()
    for copy in far:
        copy.wait_recv()
    for i in range(half):
        value = part[core * half + i, chip].astype(f32) + got_pair[i, chip].astype(f32)
        for k in range(1, chips):
            value += got_chip[k - 1, i].astype(f32)
        line_part[:, i] = value.astype(b16)
    across = []
    for k in range(1, depth):
        there = lax.rem(z + k, depth)
        across.append(send(line_part.at[there], got_line.at[k - 1], sems, base + k, line[k - 1]))
    base += depth
    for copy in across:
        copy.wait_recv()
    value = line_part[z].astype(f32)
    for k in range(1, depth):
        value += got_line[k - 1].astype(f32)
    owned[mine] = value
    swap = send(owned.at[mine], owned.at[mine], sems, base, sibling)
    base += 1
    y = y_ref[...]
    stream, rms_br, rms_st, post, final = norms(y, side_ref[...], rows)
    swap.wait_recv()
    along = owned[...] * final
    mean_st = feature_sum(stream * along)[None] / D
    dstream = rms_st * along - stream * (rms_st * rms_st * rms_st) * mean_st
    back = dstream * post
    mean_br = feature_sum(y * back)[None] / D
    dbranch = rms_br * back - y * (rms_br * rms_br * rms_br) * mean_br
    pay[:, 0] = dbranch.astype(b16)
    pay[:, 1] = dstream.astype(b16)
    home = []
    for k in range(1, chips):
        there = lax.rem(chip + k, chips) * 2 + core
        home.append(send(pay.at[there], back_ref.at[chip], sems, base + k, others[k - 1]))
    base += chips
    back_ref[chip] = pay[dp]
    for copy in home:
        copy.wait_recv()
    dy_ref[:, z] = back_ref[:, 0]
    last = []
    for k in range(1, depth):
        last.append(send(dy_ref.at[:, z], dy_ref.at[:, z], sems, base + k, line[k - 1]))
    for copy in last:
        copy.wait_recv()
    finish(first + second + list(pair.values()) + far + across + [swap] + home + last)


def head_both(chips, depth, normed, embedding, teacher, factor, local, y, side):
    count, tokens, features = normed.shape
    entries = embedding.shape[0]
    rows = y.shape[1]
    f32, b16 = jnp.float32, jnp.bfloat16
    return pl.pallas_call(
        functools.partial(head_kernel, chips, depth),
        out_shape=(
            jax.ShapeDtypeStruct((8, tokens), f32),
            jax.ShapeDtypeStruct((entries, count * features), b16),
            jax.ShapeDtypeStruct((chips, depth, rows, features), b16),
            jax.ShapeDtypeStruct((chips, 2, rows, features), b16),
        ),
        in_specs=[vmem()] * 7,
        out_specs=(vmem(),) * 4,
        scratch_shapes=[
            pltpu.VMEM((tokens, entries), f32),
            pltpu.VMEM((tokens, entries), f32),
            pltpu.VMEM((tokens, entries), f32),
            pltpu.VMEM((128, tokens), f32),
            pltpu.VMEM((8, tokens), f32),
            pltpu.VMEM((count, 8, tokens), f32),
            pltpu.VMEM((depth, 8, tokens), f32),
            pltpu.VMEM((count, entries, features), b16),
            pltpu.VMEM((count, chips, depth, rows, features), b16),
            pltpu.VMEM((chips, chips, depth, rows, features), b16),
            pltpu.VMEM((chips - 1, chips, depth, rows, features), b16),
            pltpu.VMEM((chips - 1, chips, depth, rows, features), b16),
            pltpu.VMEM((depth, chips, rows, features), b16),
            pltpu.VMEM((depth - 1, chips, rows, features), b16),
            pltpu.VMEM((count, rows, features), f32),
            pltpu.VMEM((count, 2, rows, features), b16),
            pltpu.SemaphoreType.DMA((2, 5 * chips + 3 * depth + 1)),
        ],
        compiler_params=pltpu.CompilerParams(
            collective_id=4, has_side_effects=True, vmem_limit_bytes=48 * 2**20
        ),
    )(normed, embedding, teacher, factor, local, y, side)


def input_kernel(
    chips, depth, dgate_ref, dup_ref, gate_ref, up_ref, x_ref, gain_ref, back_ref,
    out_ref, part, got, scaled, mine, inner, sems,
):
    dp, z, chip, core, group, line, others, sibling = spots(chips, depth)
    count = 2 * chips
    f32, b16 = jnp.float32, jnp.bfloat16
    rows = x_ref.shape[2]
    greet(group + line)
    dz = contract_last(dgate_ref[...], gate_ref[...]) + contract_last(dup_ref[...], up_ref[...])
    part[...] = (dz * gain_ref[0:1, :]).astype(b16).reshape(part.shape)
    base = 0
    first = []
    for k in range(1, depth):
        there = lax.rem(z + k, depth)
        first.append(send(part.at[:, there], got.at[k - 1], sems, base + k, line[k - 1]))
    base += depth
    for copy in first:
        copy.wait_recv()
    value = part[:, z].astype(f32)
    for k in range(1, depth):
        value += got[k - 1].astype(f32)
    scaled[...] = value
    x = x_ref[:, z].astype(f32)
    lane = lax.broadcasted_iota(jnp.int32, (chips, rows, 128), 2)
    products = jnp.sum(x * value, axis=2, keepdims=True)
    squares = jnp.sum(x * x, axis=2, keepdims=True)
    mine[...] = jnp.where(lane == 0, products, jnp.where(lane == 1, squares, 0.0))
    second = []
    for k in range(1, count):
        second.append(send(mine, inner.at[dp], sems, base + k, group[k - 1]))
    base += count
    inner[dp] = mine[...]
    for copy in second:
        copy.wait_recv()
    sums = jnp.sum(inner[...], axis=0)
    mean = sums[:, :, 0:1] / D / (sums[:, :, 1:2] / D + eps)
    out_ref[:, z] = (back_ref[:, 1].astype(f32) + scaled[...] - x * mean).astype(b16)
    last = []
    for k in range(1, depth):
        last.append(send(out_ref.at[:, z], out_ref.at[:, z], sems, base + k, line[k - 1]))
    for copy in last:
        copy.wait_recv()
    finish(first + second + last)


def input_backward(chips, depth, dgate, dup, gate_weight, up_weight, x_blocks, gain, back):
    _, _, rows, features = x_blocks.shape
    f32, b16 = jnp.float32, jnp.bfloat16
    return pl.pallas_call(
        functools.partial(input_kernel, chips, depth),
        out_shape=jax.ShapeDtypeStruct((chips, depth, rows, features), b16),
        in_specs=[vmem()] * 7,
        out_specs=vmem(),
        scratch_shapes=[
            pltpu.VMEM((chips, depth, rows, features), b16),
            pltpu.VMEM((depth - 1, chips, rows, features), b16),
            pltpu.VMEM((chips, rows, features), f32),
            pltpu.VMEM((chips, rows, 128), f32),
            pltpu.VMEM((2 * chips, chips, rows, 128), f32),
            pltpu.SemaphoreType.DMA((2, 2 * depth + 2 * chips)),
        ],
        compiler_params=pltpu.CompilerParams(
            collective_id=5, has_side_effects=True, vmem_limit_bytes=48 * 2**20
        ),
    )(dgate, dup, gate_weight, up_weight, x_blocks, gain, back)


def on_device(
    chips,
    depth,
    hidden_in,
    pre_gain,
    gate_weight,
    up_weight,
    down_weight,
    post_gain,
    final_gain,
    embedding,
    teacher_logits,
    target_ids,
    lengths,
):
    positions, features = hidden_in.shape
    rows = positions // (chips * depth)
    xf = hidden_in.astype(jnp.float32)
    x_gained = (xf * pre_gain).astype(jnp.bfloat16)
    square_local = jnp.sum(xf * xf, axis=1)
    h_blocks, act, slope = ffn_forward(
        chips,
        x_gained,
        jnp.broadcast_to(square_local[:, None], (positions, 128)),
        gate_weight,
        up_weight,
    )
    hidden = h_blocks.reshape(positions, -1)
    x_blocks = hidden_in.reshape(chips, depth, rows, features)
    gains = jnp.pad(jnp.stack([post_gain, final_gain]), ((0, 6), (0, 0)))
    normed, y, side, teacher = branch_forward(
        chips, depth, hidden, down_weight.T, x_blocks, gains, teacher_logits
    )
    entries = embedding.shape[0]
    mask = token_mask(lengths, positions)
    count = jnp.sum(lengths).astype(jnp.float32)
    first_entry = lax.axis_index(("dp", "vocab")) * entries
    stats, grad_emb, dy_blocks, back = head_both(
        chips,
        depth,
        normed.reshape(2 * chips, positions, features),
        embedding,
        teacher.reshape(positions, entries),
        (loss_scale / count * mask)[:, None],
        (target_ids - first_entry)[:, None],
        y,
        side,
    )
    total_s, total_t, weighted, picked = stats[0], stats[1], stats[2], stats[3]
    log_s = jnp.log(total_s)
    log_t = jnp.log(total_t)
    per_token = weighted / total_t - log_t + log_s + hard_weight * (log_s - picked)
    loss = jnp.sum(mask * per_token) / count
    grad_embedding = grad_emb
    grad_out = dy_blocks.reshape(positions, features)
    pairs = hidden_backward(chips, grad_out, down_weight.T, act, slope)
    dgate = pairs[:, :, 0].reshape(positions, -1)
    dup = pairs[:, :, 1].reshape(positions, -1)
    grad_down = contract_first(hidden, grad_out).astype(jnp.bfloat16)
    grad_gate = contract_first(x_gained, dgate).astype(jnp.bfloat16)
    grad_up = contract_first(x_gained, dup).astype(jnp.bfloat16)
    gain = jnp.broadcast_to(pre_gain[None, :], (8, features))
    grad_hidden = input_backward(
        chips, depth, dgate, dup, gate_weight, up_weight, x_blocks, gain, back
    ).reshape(positions, features)
    return (loss, grad_hidden, grad_gate, grad_up, grad_down, grad_embedding)


def pick_plan(mesh):
    chips = mesh.shape["dp"] // 2
    depth = mesh.shape["vocab"]
    tokens = LENGTH * 2
    if (
        mesh.shape["dp"] % 2 == 0
        and chips > 1
        and depth > 1
        and tokens % (32 * chips) == 0
        and tokens % (16 * chips * depth) == 0
    ):
        return functools.partial(on_device, chips, depth)
    return on_device_plain


def solution(mesh):
    return jax.shard_map(
        pick_plan(mesh),
        mesh=mesh,
        in_specs=(
            P(None, "dp"),
            P("dp"),
            P("dp", "vocab"),
            P("dp", "vocab"),
            P("vocab", "dp"),
            P("dp"),
            P("dp"),
            P(("dp", "vocab"), None),
            P("vocab", "dp"),
            P(),
            P(),
        ),
        out_specs=(
            P(),
            P(None, "dp"),
            P("dp", "vocab"),
            P("dp", "vocab"),
            P("vocab", "dp"),
            P(("dp", "vocab"), None),
        ),
        check_vma=False,
    )
```
